32 devices in a mesh: groups: 2 (over y), depth: 16 (over z, x, core).
Axes of the slice: x: 2, y: 2, z: 4, core: 2. Of those that a mesh axis runs over, the one named last changes fastest.
Arguments:
- sources: float32 [2, 8, 8, 128], P(None, 'groups'), parts along dimension 1, may hold values from -6 to 6
- plan: int32 [8], P('groups'), parts along dimension 0, may hold values from 0 to 1023
- absorb: float32 [16, 16, 128], P('depth', 'groups'), parts along dimension 1, as said below
- labels: int32 [16, 16, 128], P('depth', 'groups'), parts along dimension 1, may hold values from 0 to 7
- region_kk: float32 [8], replicated, may hold values from 0.1 to 1
- damp_cells: int32 [256], P('groups'), parts along dimension 0, may hold values from 0 to 1023
- initial_guess: float32 [2, 8, 1024, 8, 128], P(None, 'groups', 'depth'), parts along dimension 1, may hold values from -3 to 3
Outputs:
- solution: float32 [2, 8, 1024, 8, 128], P(None, 'groups', 'depth'), parts along dimension 1
The draws below stay inside these ranges and needn't reach their ends.
There are 2 independent parts, one for each index of `groups`. The reference program is written for one: setup_inputs(seed, part) draws one part's arguments, and reference() takes and returns one part's arrays. A program takes and returns all parts, laid end to end along the dimension named above; an argument that names none is the same for every part. Nothing has to cross between parts.
Inputs may be any that keep to these rules, and one draw needn't show every extreme that they name: `plan`: each source sits on one plane, counted over the whole depth. `damp_cells`: entries may repeat. `absorb`: every entry is positive.
All inputs are finite; a program needn't handle non-finite values.
Results may differ from the reference program's by a relative error of at most 0.0003.
Values sent between devices are 32-bit elements; how exact they have to be, the bound alone decides.
A program may use at most 64 MiB of HBM per device.

```python
import jax
import jax.numpy as jnp
from jax import lax

NY = 8
NZ = 128
SLAB = 64
SRC = 4
STEPS = 2
REGIONS = 8
SLAB_COUNT = 16
PLANES = 1024
NDAMP = 128


def draw_absorb(key, part):
    random_key_list = jax.random.split(jax.random.fold_in(key, 7301), 6)
    fast_share = 0.5
    pick = jax.random.uniform(random_key_list[0], (NY, NZ), jnp.float32) < fast_share
    fast_rate = jnp.exp(jax.random.uniform(random_key_list[1], (NY, NZ), jnp.float32, jnp.log(0.046), jnp.log(0.077)))
    slow_rate = jnp.exp(jax.random.uniform(random_key_list[2], (NY, NZ), jnp.float32, jnp.log(0.0004), jnp.log(0.003)))
    base = jnp.where(pick, fast_rate, slow_rate)
    jitter = jnp.exp(jax.random.uniform(random_key_list[3], (SLAB_COUNT, NY, NZ), jnp.float32, jnp.log(0.6), jnp.log(1.6)))
    grouped_slab_block = jax.random.randint(random_key_list[4], (2,), 0, SLAB_COUNT)
    source_hit_mask = jnp.any(jnp.arange(SLAB_COUNT)[:, None] == grouped_slab_block[None, :], axis=1).astype(jnp.float32)
    loss = jax.random.uniform(random_key_list[5], (SLAB_COUNT, NY, NZ), jnp.float32, 0.22, 0.69)
    return (base[None] * jitter + source_hit_mask[:, None, None] * loss).astype(jnp.float32)


def set_ends(array, stream_key, smallest, high):
    longest = array.shape.index(max(array.shape))
    spots = []
    for shift in (0, 1):
        where = [jax.random.randint(jax.random.fold_in(stream_key, axis), (), 0, length) for axis, length in enumerate(array.shape)]
        where[longest] = (where[longest] + shift) % array.shape[longest]
        spots.append(tuple(where))
    return array.at[spots[0]].set(smallest).at[spots[1]].set(high)


def block_scale(stream_key, shape, shards, low, high):
    gain = 1.0
    for position, blocks in shards:
        draws = jax.random.uniform(jax.random.fold_in(jax.random.fold_in(stream_key, 6), position), (blocks,), jnp.float32, low / len(shards), high / len(shards))
        gain = gain * jnp.repeat(jnp.exp(draws), shape[position] // blocks).reshape((-1,) + (1,) * (len(shape) - 1 - position))
    return gain


def centred(stream_key, extent, width, bound, cuts=(), kind=jnp.bfloat16):
    values = width * jax.random.normal(stream_key, extent, jnp.float32)
    if cuts:
        values = values * block_scale(stream_key, extent, cuts, -0.22, 0.18)
    return jnp.clip(values, -bound, bound).astype(kind)


def setup_inputs(seed: int = 0, part: int = 0) -> dict:
    key_of = jax.random.split(jax.random.key(seed), 8)
    part_keys = jax.random.split(jax.random.fold_in(key_of[7], part), 8)
    return {
        "sources": centred(part_keys[0], (2, SRC, NY, NZ), 1.0, 6.0, (), jnp.float32),
        "plan": set_ends(jax.random.randint(part_keys[1], (SRC,), 0, PLANES), jax.random.fold_in(part_keys[1], 1), 0, PLANES - 1).astype(jnp.int32),
        "absorb": draw_absorb(jax.random.fold_in(jax.random.fold_in(key_of[7], part), 71), part),
        "labels": set_ends(jax.random.randint(part_keys[3], (SLAB_COUNT, NY, NZ), 0, REGIONS), jax.random.fold_in(part_keys[3], 1), 0, REGIONS - 1).astype(jnp.int32),
        "region_kk": jnp.clip(jax.random.uniform(key_of[4], (REGIONS,), jnp.float32, 0.1, 1.0), 0.1, 1.0),
        "damp_cells": set_ends(jax.random.randint(part_keys[5], (NDAMP,), 0, NY * NZ), jax.random.fold_in(part_keys[5], 1), 0, (NY * NZ) - 1).astype(jnp.int32),
        "initial_guess": centred(part_keys[6], (2, SRC, PLANES, NY, NZ), 0.5, 3.0, ((2, 16),), jnp.float32),
    }


relax_weight = 0.8
shift_ratio = 0.5
damping = 3.0
coupling = 0.25

def complex_mul(left, right):
    return jnp.stack([left[0] * right[0] - left[1] * right[1], left[0] * right[1] + left[1] * right[0]])

def lateral_sum(field):
    widths = [(0, 0)] * (field.ndim - 2) + [(1, 1), (0, 0)]
    padded = jnp.pad(field, widths)
    total = padded[..., 2:, :] + padded[..., :-2, :]
    widths = [(0, 0)] * (field.ndim - 1) + [(1, 1)]
    padded = jnp.pad(field, widths)
    return total + padded[..., 2:] + padded[..., :-2]

def neighbours(extended):
    middle = extended[:, :, 1:-1]
    return extended[:, :, 2:] + extended[:, :, :-2] + lateral_sum(middle)

def pad_depth(field):
    return jnp.pad(field, ((0, 0), (0, 0), (1, 1), (0, 0), (0, 0)))

def sweep_chain(passage, emitted, backward):
    items = (jnp.moveaxis(passage, 1, 0), jnp.moveaxis(emitted, 2, 0))
    start = jnp.zeros((2, SRC, NY, NZ), jnp.float32)

    def advance(carry, item):
        return (complex_mul(item[0], carry) + item[1], carry)
    unused, seen = lax.scan(advance, start, items, reverse=backward)
    return jnp.moveaxis(seen, 0, 2)

def reference(sources, plan, absorb, labels, region_kk, damp_cells, initial_guess):
    regions = jnp.arange(REGIONS)
    squared = lax.optimization_barrier(jnp.sum(jnp.where(labels[..., None] == regions, region_kk, 0.0), axis=-1))
    cells = jnp.arange(NY * NZ)
    layer = jnp.any(damp_cells[:, None] == cells[None, :], axis=0).astype(jnp.float32).reshape(NY, NZ)
    diagonal_real_part = 6.0 - squared
    imag_diag = shift_ratio * squared + damping * layer
    complex_magnitude = diagonal_real_part * diagonal_real_part + imag_diag * imag_diag
    inverse = jnp.stack([diagonal_real_part / complex_magnitude, -imag_diag / complex_magnitude])
    orders = jnp.arange(SLAB + 1).astype(jnp.float32)[None, :, None, None]
    magnitude = jnp.exp(-orders * absorb[:, None] / SLAB)
    phase_angle_sum = orders * jnp.sqrt(squared)[:, None]
    powers = jnp.stack([magnitude * jnp.cos(phase_angle_sum), magnitude * jnp.sin(phase_angle_sum)])
    passage = powers[:, :, SLAB]
    toward_next = powers[:, :, :SLAB][:, :, ::-1][:, None]
    toward_prev = powers[:, :, :SLAB][:, None]
    entry_next = powers[:, :, 1:][:, None]
    entry_prev = powers[:, :, 1:][:, :, ::-1][:, None]
    plane_real = jnp.repeat(diagonal_real_part, SLAB, axis=0)
    inverse_planes = jnp.repeat(inverse, SLAB, axis=1)[:, None]
    planes = jnp.arange(PLANES)
    hits = (planes[None, :] == plan[:, None]).astype(jnp.float32)
    forcing = sources[:, :, None] * hits[None, :, :, None, None]
    solution = initial_guess
    for turn in range(STEPS):
        beside_all = neighbours(pad_depth(solution))
        applied = jnp.stack([plane_real * solution[0] - beside_all[0] - damping * layer * solution[1], plane_real * solution[1] - beside_all[1] + damping * layer * solution[0]])
        residual = forcing - applied
        blocks = residual.reshape(2, SRC, SLAB_COUNT, SLAB, NY, NZ)
        emit_next = lax.optimization_barrier(jnp.sum(complex_mul(toward_next, blocks), axis=3))
        emit_prev = lax.optimization_barrier(jnp.sum(complex_mul(toward_prev, blocks), axis=3))
        incoming_next = sweep_chain(passage, emit_next, False)
        incoming_prev = sweep_chain(passage, emit_prev, True)
        corrected_field = blocks + coupling * (complex_mul(entry_next, incoming_next[:, :, :, None]) + complex_mul(entry_prev, incoming_prev[:, :, :, None]))
        corrected_field = corrected_field.reshape(2, SRC, PLANES, NY, NZ)
        update = relax_weight * complex_mul(inverse_planes, corrected_field)
        for inner in range(2):
            update = (1.0 - relax_weight) * update + relax_weight * complex_mul(inverse_planes, corrected_field + neighbours(pad_depth(update)))
        solution = solution + update
    return solution
```

```python
import functools

import jax
import jax.numpy as jnp
from jax import lax
from jax.experimental import pallas as pl
from jax.experimental.pallas import tpu as pltpu
from jax.sharding import PartitionSpec as P

STEPS = 2
HALO = 3 * STEPS
CHUNK = 8

relax_weight = 0.8
shift_ratio = 0.5
damping = 3.0
coupling = 0.25


def cmul(a, b):
    return (a[0] * b[0] - a[1] * b[1], a[0] * b[1] + a[1] * b[0])


def cadd(a, b):
    return (a[0] + b[0], a[1] + b[1])


def kernel(
    n, chains_of, sources, plan, absorb, labels, kk, damp, guess, out,
    field, work, inner, power, side_next, side_prev, own, side, emits, gathered, scanned,
    incoming, passages, local_sem, halo_send, halo_recv, side_send, side_recv, pass_send,
    pass_recv, emit_send, emit_recv, scan_send, scan_recv, out_sem,
):
    me = lax.axis_index("depth")
    count = guess.shape[1]
    slab = guess.shape[2]
    height, breadth = guess.shape[3:]
    wing = HALO - 1
    chains = 2 * count

    def owner(chain):
        return (chain * n) // chains

    def slot(chain):
        return 0 if chains_of == 1 else chain

    owners = sorted({(c * n) // chains for c in range(chains)})

    barrier = pltpu.get_barrier_semaphore()

    def greet(i, _):
        pl.semaphore_signal(
            barrier, inc=1, device_id={"depth": lax.rem(me + i, n)},
            device_id_type=pl.DeviceIdType.MESH,
        )
        return 0

    lax.fori_loop(1, n, greet, 0)

    def load(s):
        return pltpu.make_async_copy(
            guess.at[:, s], field.at[s, :, pl.ds(HALO, slab)], local_sem.at[s]
        )

    for s in range(count):
        load(s).start()

    label = labels[0]
    squared = jnp.zeros((height, breadth), jnp.float32)
    for r in range(kk.shape[0]):
        squared = squared + jnp.where(label == r, kk[r], 0.0)
    rows = lax.broadcasted_iota(jnp.int32, (height, breadth), 0)
    lanes = lax.broadcasted_iota(jnp.int32, (height, breadth), 1)
    number = rows * breadth + lanes

    def mark(i, layer):
        return jnp.where(number == damp[i], 1.0, layer)

    layer = lax.fori_loop(
        0, damp.shape[0], mark, jnp.zeros((height, breadth), jnp.float32), unroll=8
    )
    own[0] = squared
    own[1] = absorb[0]

    pl.semaphore_wait(barrier, n - 1)

    def remote(src, dst, send, recv, target):
        return pltpu.make_async_remote_copy(
            src_ref=src, dst_ref=dst, send_sem=send, recv_sem=recv,
            device_id={"depth": target}, device_id_type=pl.DeviceIdType.MESH,
        )

    def side_copy(direction):
        return remote(
            own, side.at[1 - direction], side_send.at[direction], side_recv.at[1 - direction],
            me + (2 * direction - 1),
        )

    def halo_copy(s, direction):
        first = slab - HALO if direction else 0
        landing = 0 if direction else slab + HALO
        return remote(
            guess.at[:, s, pl.ds(first, HALO)], field.at[s, :, pl.ds(landing, HALO)],
            halo_send.at[s, direction], halo_recv.at[s, 1 - direction],
            me + (2 * direction - 1),
        )

    has = (me > 0, me < n - 1)
    for direction in range(2):
        @pl.when(has[direction])
        def _():
            side_copy(direction).start()
            for s in range(count):
                halo_copy(s, direction).start()

        @pl.when(jnp.logical_not(has[direction]))
        def _():
            side[direction] = jnp.zeros_like(side[direction])
            landing = slab + HALO if direction else 0
            for s in range(count):
                field[s, :, pl.ds(landing, HALO)] = jnp.zeros(
                    (2, HALO, height, breadth), jnp.float32
                )

    def wave(sq, ab):
        magnitude = jnp.exp(-ab / slab)
        phase = jnp.sqrt(sq)
        return (magnitude * jnp.cos(phase), magnitude * jnp.sin(phase))

    def relaxer(sq):
        real = 6.0 - sq
        imag = shift_ratio * sq + damping * layer
        size = real * real + imag * imag
        return (relax_weight * (real / size), relax_weight * (-imag / size))

    a_own = wave(squared, absorb[0])
    table = {0: (jnp.ones_like(squared), jnp.zeros_like(squared)), 1: a_own}
    power[0, 0], power[1, 0] = table[0]
    power[0, 1], power[1, 1] = a_own
    top = 1
    while top < slab:
        more = min(top, slab - top)
        head = (power[0, top], power[1, top])
        for j in range(1, more + 1):
            power[0, top + j], power[1, top + j] = cmul(head, (power[0, j], power[1, j]))
        top += more
    passage = (power[0, slab], power[1, slab])

    def pass_copy(i):
        return remote(
            power.at[:, slab], passages.at[me], pass_send.at[i], pass_recv, owners[i]
        )

    for i, target in enumerate(owners):
        @pl.when(me != target)
        def _():
            pass_copy(i).start()

        @pl.when(me == target)
        def _():
            passages[me, 0], passages[me, 1] = passage

    for direction in range(2):
        @pl.when(has[direction])
        def _():
            side_copy(1 - direction).wait_recv()

    damped = damping * layer
    real_own = 6.0 - squared
    g_own = relaxer(squared)
    media = []
    for direction in range(2):
        sq = side[direction, 0]
        inside = jnp.where(has[direction], 1.0, 0.0)
        g = relaxer(sq)
        a = wave(sq, side[direction, 1])

        def raised(k, a=a):
            total = None
            base = a
            while k:
                if k & 1:
                    total = base if total is None else cmul(total, base)
                k >>= 1
                if k:
                    base = cmul(base, base)
            return total

        low = a
        high = raised(slab - wing + 1)
        for i in range(wing):
            if direction == 0:
                side_next[0, 0, i], side_next[0, 1, i] = high
                side_prev[0, 0, wing - 1 - i], side_prev[0, 1, wing - 1 - i] = low
            else:
                side_next[1, 0, i], side_next[1, 1, i] = low
                side_prev[1, 0, wing - 1 - i], side_prev[1, 1, wing - 1 - i] = high
            low = cmul(low, a)
            high = cmul(high, a)
        media.append((6.0 - sq, (inside * g[0], inside * g[1])))

    keep_up, keep_down = rows > 0, rows < height - 1
    keep_left, keep_right = lanes > 0, lanes < breadth - 1

    def lateral(x):
        up = jnp.where(keep_up, pltpu.roll(x, 1, 0), 0.0)
        down = jnp.where(keep_down, pltpu.roll(x, height - 1, 0), 0.0)
        left = jnp.where(keep_left, pltpu.roll(x, 1, 1), 0.0)
        right = jnp.where(keep_right, pltpu.roll(x, breadth - 1, 1), 0.0)
        return (up + down) + (left + right)

    def window(ref, lead, first, planes):
        return [
            [ref[lead + (c, first - 1 + j)] for j in range(planes + 2)] for c in range(2)
        ]

    def beside(win, j):
        return tuple(w[j] + w[j + 2] + lateral(w[j + 1]) for w in win)

    def residual_pass(s, first, planes, real, tally):
        win = window(field, (s,), first + HALO, planes)
        source = (sources[0, s], sources[1, s])
        spot = plan[s] - me * slab
        for j in range(planes):
            value = (win[0][j + 1], win[1][j + 1])
            near = beside(win, j)
            hit = jnp.where(spot == first + j, 1.0, 0.0)
            res = (
                hit * source[0] + (near[0] - real * value[0] + damped * value[1]),
                hit * source[1] + (near[1] - real * value[1] - damped * value[0]),
            )
            work[s, 0, first + HALO + j] = res[0]
            work[s, 1, first + HALO + j] = res[1]
            if tally is not None:
                forward, backward = tally
                forward = cadd(cmul(a_own, forward), res)
                backward = cadd(
                    backward, cmul((power[0, first + j], power[1, first + j]), res)
                )
                tally = (forward, backward)
        return tally

    def start_pass(s, first, planes, g, toward, from_low, from_high):
        for j in range(planes):
            at = first + HALO + j
            up, down = toward(first + j)
            c = cadd(
                (work[s, 0, at], work[s, 1, at]), cadd(cmul(up, from_low), cmul(down, from_high))
            )
            work[s, 0, at], work[s, 1, at] = cmul(g, c)

    def middle_pass(s, first, planes, g):
        win = window(work, (s,), first + HALO, planes)
        for j in range(planes):
            at = first + HALO + j
            moved = cmul(g, beside(win, j))
            for c in range(2):
                inner[c, at] = (2.0 - relax_weight) * win[c][j + 1] + moved[c]

    def last_pass(s, first, planes, g):
        win = window(inner, (), first + HALO, planes)
        for j in range(planes):
            at = first + HALO + j
            moved = cmul(g, beside(win, j))
            for c in range(2):
                field[s, c, at] = field[s, c, at] + (
                    (1.0 - relax_weight) * win[c][j + 1] + work[s, c, at] + moved[c]
                )

    def emit_copy(t, chain):
        return remote(
            emits.at[t, chain], gathered.at[t, slot(chain), me], emit_send.at[t, chain],
            emit_recv.at[t, slot(chain)], owner(chain),
        )

    def scan_copy(t, s, direction, target):
        here = slot(2 * s + direction)
        return remote(
            scanned.at[t, here, pl.ds(target, 2)], incoming.at[t, s, direction],
            scan_send.at[t, here, target], scan_recv.at[t, s, direction], target,
        )

    def own_scan(t, s):
        for direction in range(2):
            chain = 2 * s + direction
            here = slot(chain)

            @pl.when(me == owner(chain))
            def _():
                if n > 1:
                    every = gathered.at[t, here, pl.ds(0, n - 1)]
                    pltpu.make_async_copy(every, every, emit_recv.at[t, here]).wait()
                zero = jnp.zeros((height, breadth), jnp.float32)
                edge = direction * n
                scanned[t, here, edge, 0] = zero
                scanned[t, here, edge, 1] = zero

                def one(i, state):
                    at = n - 1 - i if direction else i
                    to = at + 1 - direction
                    scanned[t, here, to, 0] = state[0]
                    scanned[t, here, to, 1] = state[1]
                    return cadd(
                        cmul((passages[at, 0], passages[at, 1]), state),
                        (gathered[t, here, at, 0], gathered[t, here, at, 1]),
                    )

                lax.fori_loop(0, n, one, (zero, zero), unroll=4)

                def give(i, _):
                    scan_copy(t, s, direction, lax.rem(me + i, n)).start()
                    return 0

                lax.fori_loop(1, n, give, 0)
                incoming[t, s, direction] = scanned[t, here, pl.ds(me, 2)]

    pieces = slab // CHUNK
    for t in range(STEPS):
        reach = 3 * (STEPS - t)

        def first_half(s, _):
            if t == 0:
                load(s).wait()
                for direction in range(2):
                    @pl.when(has[direction])
                    def _():
                        halo_copy(s, 1 - direction).wait_recv()
            zero = jnp.zeros((height, breadth), jnp.float32)
            tally = lax.fori_loop(
                0, pieces,
                lambda i, tally: residual_pass(s, i * CHUNK, CHUNK, real_own, tally),
                ((zero, zero), (zero, zero)),
            )
            for direction in range(2):
                chain = 2 * s + direction
                emits[t, chain, 0], emits[t, chain, 1] = tally[direction]

                @pl.when(me != owner(chain))
                def _():
                    emit_copy(t, chain).start()

                @pl.when(me == owner(chain))
                def _():
                    gathered[t, slot(chain), me, 0] = tally[direction][0]
                    gathered[t, slot(chain), me, 1] = tally[direction][1]
            residual_pass(s, 1 - reach, reach - 1, media[0][0], None)
            residual_pass(s, slab, reach - 1, media[1][0], None)

            @pl.when(s > 0)
            def _():
                own_scan_or_first(t, s - 1)
            return 0

        def own_scan_or_first(t, s):
            if t == 0:
                @pl.when(s == 0)
                def _():
                    for target in owners:
                        @pl.when(me == target)
                        def _():
                            if n > 1:
                                every = passages.at[pl.ds(0, n - 1)]
                                pltpu.make_async_copy(every, every, pass_recv).wait()
            own_scan(t, s)

        lax.fori_loop(0, count, first_half, 0)
        own_scan_or_first(t, jnp.int32(count - 1))

        def second_half(s, _):
            for direction in range(2):
                @pl.when(me != owner(2 * s + direction))
                def _():
                    scan_copy(t, s, direction, me).wait_recv()

            def arrived(direction, i):
                return (incoming[t, s, direction, i, 0], incoming[t, s, direction, i, 1])

            def emitted(direction):
                return (emits[t, 2 * s + direction, 0], emits[t, 2 * s + direction, 1])

            def scaled(z):
                return (coupling * z[0], coupling * z[1])

            next_low, next_own = arrived(0, 0), arrived(0, 1)
            prev_own, prev_high = arrived(1, 0), arrived(1, 1)
            next_high = scaled(cadd(cmul(passage_now(), next_own), emitted(0)))
            prev_low = scaled(cadd(cmul(passage_now(), prev_own), emitted(1)))
            next_low, next_own = scaled(next_low), scaled(next_own)
            prev_own, prev_high = scaled(prev_own), scaled(prev_high)

            def toward_own(k):
                return (
                    (power[0, k + 1], power[1, k + 1]),
                    (power[0, slab - k], power[1, slab - k]),
                )

            def toward_side(direction):
                def get(k):
                    i = k - slab if direction else k + wing
                    return (
                        (side_next[direction, 0, i], side_next[direction, 1, i]),
                        (side_prev[direction, 0, i], side_prev[direction, 1, i]),
                    )
                return get

            g_low, g_high = media[0][1], media[1][1]

            def walk(body):
                lax.fori_loop(0, pieces, lambda i, _: (body(i * CHUNK), 0)[1], 0)

            walk(lambda k: start_pass(s, k, CHUNK, g_own, toward_own, next_own, prev_own))
            start_pass(s, 1 - reach, reach - 1, g_low, toward_side(0), next_low, prev_low)
            start_pass(s, slab, reach - 1, g_high, toward_side(1), next_high, prev_high)
            walk(lambda k: middle_pass(s, k, CHUNK, g_own))
            middle_pass(s, 2 - reach, reach - 2, g_low)
            middle_pass(s, slab, reach - 2, g_high)
            walk(lambda k: last_pass(s, k, CHUNK, g_own))
            if reach > 3:
                last_pass(s, 3 - reach, reach - 3, g_low)
                last_pass(s, slab, reach - 3, g_high)
            if t == STEPS - 1:
                save(s).start()
            return 0

        def passage_now():
            return (power[0, slab], power[1, slab])

        def save(s):
            return pltpu.make_async_copy(
                field.at[s, :, pl.ds(HALO, slab)], out.at[:, s], out_sem.at[s]
            )

        lax.fori_loop(0, count, second_half, 0)

    for direction in range(2):
        @pl.when(has[direction])
        def _():
            side_copy(direction).wait_send()
            for s in range(count):
                halo_copy(s, direction).wait_send()
    for i, target in enumerate(owners):
        @pl.when(me != target)
        def _():
            pass_copy(i).wait_send()
    for t in range(STEPS):
        for chain in range(chains):
            @pl.when(me != owner(chain))
            def _():
                emit_copy(t, chain).wait_send()

            @pl.when(me == owner(chain))
            def _():
                def left(i, _):
                    scan_copy(t, chain // 2, chain % 2, lax.rem(me + i, n)).wait_send()
                    return 0

                lax.fori_loop(1, n, left, 0)
    for s in range(count):
        save(s).wait()


def local(n, sources, plan, absorb, labels, kk, damp, guess):
    count, slab, height, breadth = guess.shape[1:]
    chains = 2 * count
    slots = 1 if n >= chains else chains
    tile = (height, breadth)
    planes = slab + 2 * HALO
    f32 = jnp.float32
    dma = pltpu.SemaphoreType.DMA
    vmem = pl.BlockSpec(memory_space=pltpu.VMEM)
    smem = pl.BlockSpec(memory_space=pltpu.SMEM)
    hbm = pl.BlockSpec(memory_space=pl.ANY)
    owners = len({(c * n) // chains for c in range(chains)})
    scratch = [
        pltpu.VMEM((count, 2, planes) + tile, f32),
        pltpu.VMEM((count, 2, planes) + tile, f32),
        pltpu.VMEM((2, planes) + tile, f32),
        pltpu.VMEM((2, slab + 1) + tile, f32),
        pltpu.VMEM((2, 2, HALO - 1) + tile, f32),
        pltpu.VMEM((2, 2, HALO - 1) + tile, f32),
        pltpu.VMEM((2,) + tile, f32),
        pltpu.VMEM((2, 2) + tile, f32),
        pltpu.VMEM((STEPS, chains, 2) + tile, f32),
        pltpu.VMEM((STEPS, slots, n, 2) + tile, f32),
        pltpu.VMEM((STEPS, slots, n + 1, 2) + tile, f32),
        pltpu.VMEM((STEPS, count, 2, 2, 2) + tile, f32),
        pltpu.VMEM((n, 2) + tile, f32),
        dma((count,)),
        dma((count, 2)),
        dma((count, 2)),
        dma((2,)),
        dma((2,)),
        dma((owners,)),
        dma,
        dma((STEPS, chains)),
        dma((STEPS, slots)),
        dma((STEPS, slots, n)),
        dma((STEPS, count, 2)),
        dma((count,)),
    ]
    return pl.pallas_call(
        functools.partial(kernel, n, slots),
        out_shape=jax.ShapeDtypeStruct(guess.shape, f32),
        in_specs=[vmem, smem, vmem, vmem, smem, smem, hbm],
        out_specs=hbm,
        scratch_shapes=scratch,
        compiler_params=pltpu.CompilerParams(
            collective_id=0, has_side_effects=True, vmem_limit_bytes=48 * 2**20
        ),
        cost_estimate=pl.CostEstimate(
            flops=300 * guess.size, bytes_accessed=8 * guess.size, transcendentals=0
        ),
    )(sources, plan, absorb, labels, kk, damp, guess)


def solution(mesh):
    return jax.shard_map(
        functools.partial(local, mesh.shape["depth"]),
        mesh=mesh,
        in_specs=(
            P(None, "groups", None, None),
            P("groups"),
            P("depth", "groups", None),
            P("depth", "groups", None),
            P(),
            P("groups"),
            P(None, "groups", "depth", None, None),
        ),
        out_specs=P(None, "groups", "depth", None, None),
        check_vma=False,
    )
```

```python
import functools

import jax
import jax.numpy as jnp
from jax import lax
from jax.experimental import pallas as pl
from jax.experimental.pallas import tpu as pltpu
from jax.sharding import PartitionSpec as P

STEPS = 2
HALO = 3 * STEPS
CHUNK = 16

relax_weight = 0.8
shift_ratio = 0.5
damping = 3.0
coupling = 0.25


def cmul(a, b):
    return (a[0] * b[0] - a[1] * b[1], a[0] * b[1] + a[1] * b[0])


def cadd(a, b):
    return (a[0] + b[0], a[1] + b[1])


def kernel(
    n, chains_of, sources_in, plan_in, absorb_in, labels_in, kk_in, damp_in, guess, out,
    field, work, inner, power, side_next, side_prev, own, side, emits, gathered, scanned,
    incoming, passages, sources, plan, absorb, labels, kk, damp, arg_sem, local_sem, halo_send, halo_recv, side_send, side_recv, pass_send,
    pass_recv, emit_send, emit_recv, scan_send, scan_recv, out_sem,
):
    me = lax.axis_index("depth")
    count = guess.shape[1]
    slab = guess.shape[2]
    height, breadth = guess.shape[3:]
    wing = HALO - 1
    chains = 2 * count

    def owner(chain):
        return (chain * n) // chains

    def slot(chain):
        return 0 if chains_of == 1 else chain

    owners = sorted({(c * n) // chains for c in range(chains)})

    barrier = pltpu.get_barrier_semaphore()

    def greet(i, _):
        pl.semaphore_signal(
            barrier, inc=1, device_id={"depth": lax.rem(me + i, n)},
            device_id_type=pl.DeviceIdType.MESH,
        )
        return 0

    lax.fori_loop(1, n, greet, 0)

    def load(s):
        return pltpu.make_async_copy(
            guess.at[:, s], field.at[s, :, pl.ds(HALO, slab)], local_sem.at[s]
        )

    fetches = [
        pltpu.make_async_copy(there, here, arg_sem.at[i])
        for i, (there, here) in enumerate(
            (
                (labels_in, labels), (kk_in, kk), (damp_in, damp), (absorb_in, absorb),
                (plan_in, plan), (sources_in, sources),
            )
        )
    ]
    for fetch in fetches:
        fetch.start()
    for s in range(count):
        load(s).start()
    for fetch in fetches:
        fetch.wait()

    label = labels[0]
    squared = jnp.zeros((height, breadth), jnp.float32)
    for r in range(kk.shape[0]):
        squared = squared + jnp.where(label == r, kk[r], 0.0)
    rows = lax.broadcasted_iota(jnp.int32, (height, breadth), 0)
    lanes = lax.broadcasted_iota(jnp.int32, (height, breadth), 1)
    number = rows * breadth + lanes

    def mark(i, layer):
        return jnp.where(number == damp[i], 1.0, layer)

    layer = lax.fori_loop(
        0, damp.shape[0], mark, jnp.zeros((height, breadth), jnp.float32), unroll=8
    )
    own[0] = squared
    own[1] = absorb[0]

    pl.semaphore_wait(barrier, n - 1)

    def remote(src, dst, send, recv, target):
        return pltpu.make_async_remote_copy(
            src_ref=src, dst_ref=dst, send_sem=send, recv_sem=recv,
            device_id={"depth": target}, device_id_type=pl.DeviceIdType.MESH,
        )

    def side_copy(direction):
        return remote(
            own, side.at[1 - direction], side_send.at[direction], side_recv.at[1 - direction],
            me + (2 * direction - 1),
        )

    def halo_copy(s, direction):
        first = slab - HALO if direction else 0
        landing = 0 if direction else slab + HALO
        return remote(
            guess.at[:, s, pl.ds(first, HALO)], field.at[s, :, pl.ds(landing, HALO)],
            halo_send.at[s, direction], halo_recv.at[s, 1 - direction],
            me + (2 * direction - 1),
        )

    has = (me > 0, me < n - 1)
    for direction in range(2):
        @pl.when(has[direction])
        def _():
            side_copy(direction).start()
            for s in range(count):
                halo_copy(s, direction).start()

        @pl.when(jnp.logical_not(has[direction]))
        def _():
            side[direction] = jnp.zeros_like(side[direction])
            landing = slab + HALO if direction else 0
            for s in range(count):
                field[s, :, pl.ds(landing, HALO)] = jnp.zeros(
                    (2, HALO, height, breadth), jnp.float32
                )

    def wave(sq, ab):
        magnitude = jnp.exp(-ab / slab)
        phase = jnp.sqrt(sq)
        return (magnitude * jnp.cos(phase), magnitude * jnp.sin(phase))

    def relaxer(sq):
        real = 6.0 - sq
        imag = shift_ratio * sq + damping * layer
        size = real * real + imag * imag
        return (relax_weight * (real / size), relax_weight * (-imag / size))

    a_own = wave(squared, absorb[0])
    table = {0: (jnp.ones_like(squared), jnp.zeros_like(squared)), 1: a_own}
    power[0, 0], power[1, 0] = table[0]
    power[0, 1], power[1, 1] = a_own
    top = 1
    while top < slab:
        more = min(top, slab - top)
        head = (power[0, top], power[1, top])
        for j in range(1, more + 1):
            power[0, top + j], power[1, top + j] = cmul(head, (power[0, j], power[1, j]))
        top += more
    passage = (power[0, slab], power[1, slab])

    def pass_copy(i):
        return remote(
            power.at[:, slab], passages.at[me], pass_send.at[i], pass_recv, owners[i]
        )

    for i, target in enumerate(owners):
        @pl.when(me != target)
        def _():
            pass_copy(i).start()

        @pl.when(me == target)
        def _():
            passages[me, 0], passages[me, 1] = passage

    for direction in range(2):
        @pl.when(has[direction])
        def _():
            side_copy(1 - direction).wait_recv()

    damped = damping * layer
    real_own = 6.0 - squared
    g_own = relaxer(squared)
    media = []
    for direction in range(2):
        sq = side[direction, 0]
        inside = jnp.where(has[direction], 1.0, 0.0)
        g = relaxer(sq)
        a = wave(sq, side[direction, 1])

        def raised(k, a=a):
            total = None
            base = a
            while k:
                if k & 1:
                    total = base if total is None else cmul(total, base)
                k >>= 1
                if k:
                    base = cmul(base, base)
            return total

        low = a
        high = raised(slab - wing + 1)
        for i in range(wing):
            if direction == 0:
                side_next[0, 0, i], side_next[0, 1, i] = high
                side_prev[0, 0, wing - 1 - i], side_prev[0, 1, wing - 1 - i] = low
            else:
                side_next[1, 0, i], side_next[1, 1, i] = low
                side_prev[1, 0, wing - 1 - i], side_prev[1, 1, wing - 1 - i] = high
            low = cmul(low, a)
            high = cmul(high, a)
        media.append((6.0 - sq, (inside * g[0], inside * g[1])))

    keep_up, keep_down = rows > 0, rows < height - 1
    keep_left, keep_right = lanes > 0, lanes < breadth - 1

    def lateral(x):
        up = jnp.where(keep_up, pltpu.roll(x, 1, 0), 0.0)
        down = jnp.where(keep_down, pltpu.roll(x, height - 1, 0), 0.0)
        left = jnp.where(keep_left, pltpu.roll(x, 1, 1), 0.0)
        right = jnp.where(keep_right, pltpu.roll(x, breadth - 1, 1), 0.0)
        return (up + down) + (left + right)

    def window(ref, lead, first, planes):
        return [
            [ref[lead + (c, first - 1 + j)] for j in range(planes + 2)] for c in range(2)
        ]

    def beside(win, j):
        return tuple(w[j] + w[j + 2] + lateral(w[j + 1]) for w in win)

    def residual_pass(s, first, planes, real, tally):
        win = window(field, (s,), first + HALO, planes)
        source = (sources[0, s], sources[1, s])
        spot = plan[s] - me * slab
        results = []
        for j in range(planes):
            value = (win[0][j + 1], win[1][j + 1])
            near = beside(win, j)
            hit = jnp.where(spot == first + j, 1.0, 0.0)
            res = (
                hit * source[0] + (near[0] - real * value[0] + damped * value[1]),
                hit * source[1] + (near[1] - real * value[1] - damped * value[0]),
            )
            results.append(res)
            if tally is not None:
                forward, backward = tally
                forward = cadd(cmul(a_own, forward), res)
                backward = cadd(
                    backward, cmul((power[0, first + j], power[1, first + j]), res)
                )
                tally = (forward, backward)
        for j in range(planes):
            for c in range(2):
                work[s, c, first + HALO + j] = results[j][c]
        return tally

    def start_pass(s, first, planes, g, toward, from_low, from_high):
        lead = first + HALO
        held = [(work[s, 0, lead + j], work[s, 1, lead + j]) for j in range(planes)]
        results = []
        for j in range(planes):
            up, down = toward(first + j)
            c = cadd(held[j], cadd(cmul(up, from_low), cmul(down, from_high)))
            results.append(cmul(g, c))
        for j in range(planes):
            work[s, 0, lead + j], work[s, 1, lead + j] = results[j]

    def middle_pass(s, first, planes, g):
        lead = first + HALO
        win = window(work, (s,), lead, planes)
        results = []
        for j in range(planes):
            moved = cmul(g, beside(win, j))
            results.append(
                [(2.0 - relax_weight) * win[c][j + 1] + moved[c] for c in range(2)]
            )
        for j in range(planes):
            inner[0, lead + j], inner[1, lead + j] = results[j]

    def last_pass(s, first, planes, g):
        lead = first + HALO
        win = window(inner, (), lead, planes)
        held = [
            [field[s, c, lead + j] + work[s, c, lead + j] for c in range(2)]
            for j in range(planes)
        ]
        results = []
        for j in range(planes):
            moved = cmul(g, beside(win, j))
            results.append(
                [
                    held[j][c] + ((1.0 - relax_weight) * win[c][j + 1] + moved[c])
                    for c in range(2)
                ]
            )
        for j in range(planes):
            field[s, 0, lead + j], field[s, 1, lead + j] = results[j]

    def emit_copy(t, chain):
        return remote(
            emits.at[t, chain], gathered.at[t, slot(chain), me], emit_send.at[t, chain],
            emit_recv.at[t, slot(chain)], owner(chain),
        )

    def scan_copy(t, s, direction, target):
        here = slot(2 * s + direction)
        return remote(
            scanned.at[t, here, pl.ds(target, 2)], incoming.at[t, s, direction],
            scan_send.at[t, here, target], scan_recv.at[t, s, direction], target,
        )

    def own_scan(t, s):
        for direction in range(2):
            chain = 2 * s + direction
            here = slot(chain)

            @pl.when(me == owner(chain))
            def _():
                if n > 1:
                    every = gathered.at[t, here, pl.ds(0, n - 1)]
                    pltpu.make_async_copy(every, every, emit_recv.at[t, here]).wait()
                zero = jnp.zeros((height, breadth), jnp.float32)
                edge = direction * n
                scanned[t, here, edge, 0] = zero
                scanned[t, here, edge, 1] = zero

                def one(i, state):
                    at = n - 1 - i if direction else i
                    to = at + 1 - direction
                    scanned[t, here, to, 0] = state[0]
                    scanned[t, here, to, 1] = state[1]
                    return cadd(
                        cmul((passages[at, 0], passages[at, 1]), state),
                        (gathered[t, here, at, 0], gathered[t, here, at, 1]),
                    )

                lax.fori_loop(0, n, one, (zero, zero), unroll=4)

                def give(i, _):
                    scan_copy(t, s, direction, lax.rem(me + i, n)).start()
                    return 0

                lax.fori_loop(1, n, give, 0)
                incoming[t, s, direction] = scanned[t, here, pl.ds(me, 2)]

    pieces = slab // CHUNK
    for t in range(STEPS):
        reach = 3 * (STEPS - t)

        def first_half(s, _):
            if t == 0:
                load(s).wait()
                for direction in range(2):
                    @pl.when(has[direction])
                    def _():
                        halo_copy(s, 1 - direction).wait_recv()
            zero = jnp.zeros((height, breadth), jnp.float32)
            tally = lax.fori_loop(
                0, pieces,
                lambda i, tally: residual_pass(s, i * CHUNK, CHUNK, real_own, tally),
                ((zero, zero), (zero, zero)),
            )
            for direction in range(2):
                chain = 2 * s + direction
                emits[t, chain, 0], emits[t, chain, 1] = tally[direction]

                @pl.when(me != owner(chain))
                def _():
                    emit_copy(t, chain).start()

                @pl.when(me == owner(chain))
                def _():
                    gathered[t, slot(chain), me, 0] = tally[direction][0]
                    gathered[t, slot(chain), me, 1] = tally[direction][1]
            residual_pass(s, 1 - reach, reach - 1, media[0][0], None)
            residual_pass(s, slab, reach - 1, media[1][0], None)

            @pl.when(s > 0)
            def _():
                own_scan_or_first(t, s - 1)
            return 0

        def own_scan_or_first(t, s):
            if t == 0:
                @pl.when(s == 0)
                def _():
                    for target in owners:
                        @pl.when(me == target)
                        def _():
                            if n > 1:
                                every = passages.at[pl.ds(0, n - 1)]
                                pltpu.make_async_copy(every, every, pass_recv).wait()
            own_scan(t, s)

        lax.fori_loop(0, count, first_half, 0)
        own_scan_or_first(t, jnp.int32(count - 1))

        def second_half(s, _):
            for direction in range(2):
                @pl.when(me != owner(2 * s + direction))
                def _():
                    scan_copy(t, s, direction, me).wait_recv()

            def arrived(direction, i):
                return (incoming[t, s, direction, i, 0], incoming[t, s, direction, i, 1])

            def emitted(direction):
                return (emits[t, 2 * s + direction, 0], emits[t, 2 * s + direction, 1])

            def scaled(z):
                return (coupling * z[0], coupling * z[1])

            next_low, next_own = arrived(0, 0), arrived(0, 1)
            prev_own, prev_high = arrived(1, 0), arrived(1, 1)
            next_high = scaled(cadd(cmul(passage_now(), next_own), emitted(0)))
            prev_low = scaled(cadd(cmul(passage_now(), prev_own), emitted(1)))
            next_low, next_own = scaled(next_low), scaled(next_own)
            prev_own, prev_high = scaled(prev_own), scaled(prev_high)

            def toward_own(k):
                return (
                    (power[0, k + 1], power[1, k + 1]),
                    (power[0, slab - k], power[1, slab - k]),
                )

            def toward_side(direction):
                def get(k):
                    i = k - slab if direction else k + wing
                    return (
                        (side_next[direction, 0, i], side_next[direction, 1, i]),
                        (side_prev[direction, 0, i], side_prev[direction, 1, i]),
                    )
                return get

            g_low, g_high = media[0][1], media[1][1]

            def walk(body):
                lax.fori_loop(0, pieces, lambda i, _: (body(i * CHUNK), 0)[1], 0)

            walk(lambda k: start_pass(s, k, CHUNK, g_own, toward_own, next_own, prev_own))
            start_pass(s, 1 - reach, reach - 1, g_low, toward_side(0), next_low, prev_low)
            start_pass(s, slab, reach - 1, g_high, toward_side(1), next_high, prev_high)
            walk(lambda k: middle_pass(s, k, CHUNK, g_own))
            middle_pass(s, 2 - reach, reach - 2, g_low)
            middle_pass(s, slab, reach - 2, g_high)
            walk(lambda k: last_pass(s, k, CHUNK, g_own))
            if reach > 3:
                last_pass(s, 3 - reach, reach - 3, g_low)
                last_pass(s, slab, reach - 3, g_high)
            if t == STEPS - 1:
                save(s).start()
            return 0

        def passage_now():
            return (power[0, slab], power[1, slab])

        def save(s):
            return pltpu.make_async_copy(
                field.at[s, :, pl.ds(HALO, slab)], out.at[:, s], out_sem.at[s]
            )

        lax.fori_loop(0, count, second_half, 0)

    for direction in range(2):
        @pl.when(has[direction])
        def _():
            side_copy(direction).wait_send()
            for s in range(count):
                halo_copy(s, direction).wait_send()
    for i, target in enumerate(owners):
        @pl.when(me != target)
        def _():
            pass_copy(i).wait_send()
    for t in range(STEPS):
        for chain in range(chains):
            @pl.when(me != owner(chain))
            def _():
                emit_copy(t, chain).wait_send()

            @pl.when(me == owner(chain))
            def _():
                def left(i, _):
                    scan_copy(t, chain // 2, chain % 2, lax.rem(me + i, n)).wait_send()
                    return 0

                lax.fori_loop(1, n, left, 0)
    for s in range(count):
        save(s).wait()


def local(n, sources, plan, absorb, labels, kk, damp, guess):
    count, slab, height, breadth = guess.shape[1:]
    chains = 2 * count
    slots = 1 if n >= chains else chains
    tile = (height, breadth)
    planes = slab + 2 * HALO
    f32 = jnp.float32
    dma = pltpu.SemaphoreType.DMA
    hbm = pl.BlockSpec(memory_space=pl.ANY)
    owners = len({(c * n) // chains for c in range(chains)})
    scratch = [
        pltpu.VMEM((count, 2, planes) + tile, f32),
        pltpu.VMEM((count, 2, planes) + tile, f32),
        pltpu.VMEM((2, planes) + tile, f32),
        pltpu.VMEM((2, slab + 1) + tile, f32),
        pltpu.VMEM((2, 2, HALO - 1) + tile, f32),
        pltpu.VMEM((2, 2, HALO - 1) + tile, f32),
        pltpu.VMEM((2,) + tile, f32),
        pltpu.VMEM((2, 2) + tile, f32),
        pltpu.VMEM((STEPS, chains, 2) + tile, f32),
        pltpu.VMEM((STEPS, slots, n, 2) + tile, f32),
        pltpu.VMEM((STEPS, slots, n + 1, 2) + tile, f32),
        pltpu.VMEM((STEPS, count, 2, 2, 2) + tile, f32),
        pltpu.VMEM((n, 2) + tile, f32),
        pltpu.VMEM(sources.shape, f32),
        pltpu.SMEM(plan.shape, jnp.int32),
        pltpu.VMEM(absorb.shape, f32),
        pltpu.VMEM(labels.shape, jnp.int32),
        pltpu.SMEM(kk.shape, f32),
        pltpu.SMEM(damp.shape, jnp.int32),
        dma((6,)),
        dma((count,)),
        dma((count, 2)),
        dma((count, 2)),
        dma((2,)),
        dma((2,)),
        dma((owners,)),
        dma,
        dma((STEPS, chains)),
        dma((STEPS, slots)),
        dma((STEPS, slots, n)),
        dma((STEPS, count, 2)),
        dma((count,)),
    ]
    return pl.pallas_call(
        functools.partial(kernel, n, slots),
        out_shape=jax.ShapeDtypeStruct(guess.shape, f32),
        in_specs=[hbm] * 7,
        out_specs=hbm,
        scratch_shapes=scratch,
        compiler_params=pltpu.CompilerParams(
            collective_id=0, has_side_effects=True, vmem_limit_bytes=60 * 2**20
        ),
        cost_estimate=pl.CostEstimate(
            flops=300 * guess.size, bytes_accessed=8 * guess.size, transcendentals=0
        ),
    )(sources, plan, absorb, labels, kk, damp, guess)


def solution(mesh):
    return jax.shard_map(
        functools.partial(local, mesh.shape["depth"]),
        mesh=mesh,
        in_specs=(
            P(None, "groups", None, None),
            P("groups"),
            P("depth", "groups", None),
            P("depth", "groups", None),
            P(),
            P("groups"),
            P(None, "groups", "depth", None, None),
        ),
        out_specs=P(None, "groups", "depth", None, None),
        check_vma=False,
    )
```

```python
import functools

import jax
import jax.numpy as jnp
from jax import lax
from jax.experimental import pallas as pl
from jax.experimental.pallas import tpu as pltpu
from jax.sharding import PartitionSpec as P

STEPS = 2
HALO = 3 * STEPS
CHUNK = 32

relax_weight = 0.8
shift_ratio = 0.5
damping = 3.0
coupling = 0.25


def cmul(a, b):
    return (a[0] * b[0] - a[1] * b[1], a[0] * b[1] + a[1] * b[0])


def cadd(a, b):
    return (a[0] + b[0], a[1] + b[1])


def kernel(
    n, chains_of, sources_in, plan_in, absorb_in, labels_in, kk_in, damp_in, guess, out,
    field, work, inner, power, side_next, side_prev, own, side, emits, gathered, scanned,
    incoming, passages, sources, plan, absorb, labels, kk, damp, arg_sem, local_sem, halo_send, halo_recv, side_send, side_recv, pass_send,
    pass_recv, emit_send, emit_recv, scan_send, scan_recv,
):
    me = lax.axis_index("depth")
    count = guess.shape[1]
    slab = guess.shape[2]
    height, breadth = guess.shape[3:]
    wing = HALO - 1
    chains = 2 * count

    def owner(chain):
        return (chain * n) // chains

    def slot(chain):
        return 0 if chains_of == 1 else chain

    owners = sorted({(c * n) // chains for c in range(chains)})

    barrier = pltpu.get_barrier_semaphore()

    def greet(i, _):
        pl.semaphore_signal(
            barrier, inc=1, device_id={"depth": lax.rem(me + i, n)},
            device_id_type=pl.DeviceIdType.MESH,
        )
        return 0

    lax.fori_loop(1, n, greet, 0)

    def load(s):
        return pltpu.make_async_copy(
            guess.at[:, s], field.at[s, :, pl.ds(HALO, slab)], local_sem.at[s]
        )

    fetches = [
        pltpu.make_async_copy(there, here, arg_sem.at[i])
        for i, (there, here) in enumerate(
            (
                (labels_in, labels), (kk_in, kk), (damp_in, damp), (absorb_in, absorb),
                (plan_in, plan), (sources_in, sources),
            )
        )
    ]
    for fetch in fetches:
        fetch.start()
    for s in range(count):
        load(s).start()
    for fetch in fetches:
        fetch.wait()

    label = labels[0]
    squared = jnp.zeros((height, breadth), jnp.float32)
    for r in range(kk.shape[0]):
        squared = squared + jnp.where(label == r, kk[r], 0.0)
    rows = lax.broadcasted_iota(jnp.int32, (height, breadth), 0)
    lanes = lax.broadcasted_iota(jnp.int32, (height, breadth), 1)
    number = rows * breadth + lanes

    def mark(i, layer):
        return jnp.where(number == damp[i], 1.0, layer)

    layer = lax.fori_loop(
        0, damp.shape[0], mark, jnp.zeros((height, breadth), jnp.float32), unroll=8
    )
    own[0] = squared
    own[1] = absorb[0]

    pl.semaphore_wait(barrier, n - 1)

    def remote(src, dst, send, recv, target):
        return pltpu.make_async_remote_copy(
            src_ref=src, dst_ref=dst, send_sem=send, recv_sem=recv,
            device_id={"depth": target}, device_id_type=pl.DeviceIdType.MESH,
        )

    def side_copy(direction):
        return remote(
            own, side.at[1 - direction], side_send.at[direction], side_recv.at[1 - direction],
            me + (2 * direction - 1),
        )

    def halo_copy(s, direction):
        first = slab - HALO if direction else 0
        landing = 0 if direction else slab + HALO
        return remote(
            guess.at[:, s, pl.ds(first, HALO)], field.at[s, :, pl.ds(landing, HALO)],
            halo_send.at[s, direction], halo_recv.at[s, 1 - direction],
            me + (2 * direction - 1),
        )

    has = (me > 0, me < n - 1)
    for direction in range(2):
        @pl.when(has[direction])
        def _():
            side_copy(direction).start()
            for s in range(count):
                halo_copy(s, direction).start()

        @pl.when(jnp.logical_not(has[direction]))
        def _():
            side[direction] = jnp.zeros_like(side[direction])
            landing = slab + HALO if direction else 0
            for s in range(count):
                field[s, :, pl.ds(landing, HALO)] = jnp.zeros(
                    (2, HALO, height, breadth), jnp.float32
                )

    def wave(sq, ab):
        magnitude = jnp.exp(-ab / slab)
        phase = jnp.sqrt(sq)
        return (magnitude * jnp.cos(phase), magnitude * jnp.sin(phase))

    def relaxer(sq):
        real = 6.0 - sq
        imag = shift_ratio * sq + damping * layer
        size = real * real + imag * imag
        return (relax_weight * (real / size), relax_weight * (-imag / size))

    a_own = wave(squared, absorb[0])
    table = {0: (jnp.ones_like(squared), jnp.zeros_like(squared)), 1: a_own}
    power[0, 0], power[1, 0] = table[0]
    power[0, 1], power[1, 1] = a_own
    top = 1
    while top < slab:
        more = min(top, slab - top)
        head = (power[0, top], power[1, top])
        for j in range(1, more + 1):
            power[0, top + j], power[1, top + j] = cmul(head, (power[0, j], power[1, j]))
        top += more
    passage = (power[0, slab], power[1, slab])

    def pass_copy(i):
        return remote(
            power.at[:, slab], passages.at[me], pass_send.at[i], pass_recv, owners[i]
        )

    for i, target in enumerate(owners):
        @pl.when(me != target)
        def _():
            pass_copy(i).start()

        @pl.when(me == target)
        def _():
            passages[me, 0], passages[me, 1] = passage

    for direction in range(2):
        @pl.when(has[direction])
        def _():
            side_copy(1 - direction).wait_recv()

    damped = damping * layer
    real_own = 6.0 - squared
    g_own = relaxer(squared)
    media = []
    for direction in range(2):
        sq = side[direction, 0]
        inside = jnp.where(has[direction], 1.0, 0.0)
        g = relaxer(sq)
        a = wave(sq, side[direction, 1])

        def raised(k, a=a):
            total = None
            base = a
            while k:
                if k & 1:
                    total = base if total is None else cmul(total, base)
                k >>= 1
                if k:
                    base = cmul(base, base)
            return total

        low = a
        high = raised(slab - wing + 1)
        for i in range(wing):
            if direction == 0:
                side_next[0, 0, i], side_next[0, 1, i] = high
                side_prev[0, 0, wing - 1 - i], side_prev[0, 1, wing - 1 - i] = low
            else:
                side_next[1, 0, i], side_next[1, 1, i] = low
                side_prev[1, 0, wing - 1 - i], side_prev[1, 1, wing - 1 - i] = high
            low = cmul(low, a)
            high = cmul(high, a)
        media.append((6.0 - sq, (inside * g[0], inside * g[1])))

    keep_up, keep_down = rows > 0, rows < height - 1
    keep_left, keep_right = lanes > 0, lanes < breadth - 1

    def lateral(x):
        up = jnp.where(keep_up, pltpu.roll(x, 1, 0), 0.0)
        down = jnp.where(keep_down, pltpu.roll(x, height - 1, 0), 0.0)
        left = jnp.where(keep_left, pltpu.roll(x, 1, 1), 0.0)
        right = jnp.where(keep_right, pltpu.roll(x, breadth - 1, 1), 0.0)
        return (up + down) + (left + right)

    def window(ref, lead, first, planes):
        return [
            [ref[lead + (c, first - 1 + j)] for j in range(planes + 2)] for c in range(2)
        ]

    def beside(win, j):
        return tuple(w[j] + w[j + 2] + lateral(w[j + 1]) for w in win)

    def residual_pass(s, parts, tally):
        wins = [window(field, (s,), part[0] + HALO, part[1]) for part in parts]
        source = (sources[0, s], sources[1, s])
        spot = plan[s] - me * slab
        results = []
        for (first, planes, real), win in zip(parts, wins):
            for j in range(planes):
                value = (win[0][j + 1], win[1][j + 1])
                near = beside(win, j)
                hit = jnp.where(spot == first + j, 1.0, 0.0)
                res = (
                    hit * source[0] + (near[0] - real * value[0] + damped * value[1]),
                    hit * source[1] + (near[1] - real * value[1] - damped * value[0]),
                )
                results.append((first + HALO + j, res))
                if tally is not None:
                    k = first + j
                    ahead = (power[0, slab - 1 - k], power[1, slab - 1 - k])
                    behind = (power[0, k], power[1, k])
                    tally = (
                        cadd(tally[0], cmul(ahead, res)), cadd(tally[1], cmul(behind, res))
                    )
        for at, res in results:
            work[s, 0, at], work[s, 1, at] = res
        return tally

    def start_pass(s, parts):
        results = []
        for first, planes, g, toward, from_low, from_high in parts:
            for j in range(planes):
                at = first + HALO + j
                up, down = toward(first + j)
                c = cadd(
                    (work[s, 0, at], work[s, 1, at]),
                    cadd(cmul(up, from_low), cmul(down, from_high)),
                )
                results.append((at, cmul(g, c)))
        for at, value in results:
            work[s, 0, at], work[s, 1, at] = value

    def middle_pass(s, parts):
        wins = [window(work, (s,), part[0] + HALO, part[1]) for part in parts]
        results = []
        for (first, planes, g), win in zip(parts, wins):
            for j in range(planes):
                moved = cmul(g, beside(win, j))
                results.append(
                    (
                        first + HALO + j,
                        [(2.0 - relax_weight) * win[c][j + 1] + moved[c] for c in range(2)],
                    )
                )
        for at, value in results:
            inner[0, at], inner[1, at] = value

    def last_pass(s, parts, final):
        wins = [window(inner, (), part[0] + HALO, part[1]) for part in parts]
        results = []
        for (first, planes, g), win in zip(parts, wins):
            for j in range(planes):
                at = first + HALO + j
                moved = cmul(g, beside(win, j))
                results.append(
                    (
                        first + j,
                        [
                            (field[s, c, at] + work[s, c, at])
                            + ((1.0 - relax_weight) * win[c][j + 1] + moved[c])
                            for c in range(2)
                        ],
                    )
                )
        for at, value in results:
            field[s, 0, at + HALO], field[s, 1, at + HALO] = value
            if final:
                out[0, s, at], out[1, s, at] = value

    def emit_copy(t, chain):
        return remote(
            emits.at[t, chain], gathered.at[t, slot(chain), me], emit_send.at[t, chain],
            emit_recv.at[t, slot(chain)], owner(chain),
        )

    def scan_copy(t, s, direction, target):
        here = slot(2 * s + direction)
        return remote(
            scanned.at[t, here, pl.ds(target, 2)], incoming.at[t, s, direction],
            scan_send.at[t, here, target], scan_recv.at[t, s, direction], target,
        )

    def own_scan(t, s):
        for direction in range(2):
            chain = 2 * s + direction
            here = slot(chain)

            @pl.when(me == owner(chain))
            def _():
                if n > 1:
                    every = gathered.at[t, here, pl.ds(0, n - 1)]
                    pltpu.make_async_copy(every, every, emit_recv.at[t, here]).wait()
                zero = jnp.zeros((height, breadth), jnp.float32)
                edge = direction * n
                scanned[t, here, edge, 0] = zero
                scanned[t, here, edge, 1] = zero

                def one(i, state):
                    at = n - 1 - i if direction else i
                    to = at + 1 - direction
                    scanned[t, here, to, 0] = state[0]
                    scanned[t, here, to, 1] = state[1]
                    return cadd(
                        cmul((passages[at, 0], passages[at, 1]), state),
                        (gathered[t, here, at, 0], gathered[t, here, at, 1]),
                    )

                lax.fori_loop(0, n, one, (zero, zero), unroll=4)

                def give(i, _):
                    scan_copy(t, s, direction, lax.rem(me + i, n)).start()
                    return 0

                lax.fori_loop(1, n, give, 0)
                incoming[t, s, direction] = scanned[t, here, pl.ds(me, 2)]

    pieces = slab // CHUNK
    units = STEPS * count

    def at_step(t, body):
        for step in range(STEPS):
            @pl.when(t == step)
            def _():
                body(3 * (STEPS - step))

    def first_half(t, s):
        @pl.when(t == 0)
        def _():
            load(s).wait()
            for direction in range(2):
                @pl.when(has[direction])
                def _():
                    halo_copy(s, 1 - direction).wait_recv()

        zero = jnp.zeros((height, breadth), jnp.float32)
        tally = lax.fori_loop(
            0, pieces,
            lambda i, tally: residual_pass(s, [(i * CHUNK, CHUNK, real_own)], tally),
            ((zero, zero), (zero, zero)),
        )
        for direction in range(2):
            chain = 2 * s + direction
            emits[t, chain, 0], emits[t, chain, 1] = tally[direction]

            @pl.when(me != owner(chain))
            def _():
                emit_copy(t, chain).start()

            @pl.when(me == owner(chain))
            def _():
                gathered[t, slot(chain), me, 0] = tally[direction][0]
                gathered[t, slot(chain), me, 1] = tally[direction][1]

        def sides(reach):
            residual_pass(
                s, [(1 - reach, reach - 1, media[0][0]), (slab, reach - 1, media[1][0])], None
            )

        at_step(t, sides)

    def passages_here():
        for target in owners:
            @pl.when(me == target)
            def _():
                if n > 1:
                    every = passages.at[pl.ds(0, n - 1)]
                    pltpu.make_async_copy(every, every, pass_recv).wait()

    def second_half(t, s):
        for direction in range(2):
            @pl.when(me != owner(2 * s + direction))
            def _():
                scan_copy(t, s, direction, me).wait_recv()

        def arrived(direction, i):
            return (incoming[t, s, direction, i, 0], incoming[t, s, direction, i, 1])

        def emitted(direction):
            return (emits[t, 2 * s + direction, 0], emits[t, 2 * s + direction, 1])

        def scaled(z):
            return (coupling * z[0], coupling * z[1])

        through = (power[0, slab], power[1, slab])
        next_low, next_own = arrived(0, 0), arrived(0, 1)
        prev_own, prev_high = arrived(1, 0), arrived(1, 1)
        next_high = scaled(cadd(cmul(through, next_own), emitted(0)))
        prev_low = scaled(cadd(cmul(through, prev_own), emitted(1)))
        next_low, next_own = scaled(next_low), scaled(next_own)
        prev_own, prev_high = scaled(prev_own), scaled(prev_high)

        def toward_own(k):
            return (
                (power[0, k + 1], power[1, k + 1]),
                (power[0, slab - k], power[1, slab - k]),
            )

        def toward_side(direction):
            def get(k):
                i = k - slab if direction else k + wing
                return (
                    (side_next[direction, 0, i], side_next[direction, 1, i]),
                    (side_prev[direction, 0, i], side_prev[direction, 1, i]),
                )
            return get

        g_low, g_high = media[0][1], media[1][1]

        def walk(body):
            lax.fori_loop(0, pieces, lambda i, _: (body(i * CHUNK), 0)[1], 0)

        walk(
            lambda k: start_pass(s, [(k, CHUNK, g_own, toward_own, next_own, prev_own)])
        )

        def start_sides(reach):
            start_pass(
                s,
                [
                    (1 - reach, reach - 1, g_low, toward_side(0), next_low, prev_low),
                    (slab, reach - 1, g_high, toward_side(1), next_high, prev_high),
                ],
            )
            middle_pass(s, [(2 - reach, reach - 2, g_low), (slab, reach - 2, g_high)])

        at_step(t, start_sides)
        walk(lambda k: middle_pass(s, [(k, CHUNK, g_own)]))
        walk(lambda k: last_pass(s, [(k, CHUNK, g_own)], True))

        def last_sides(reach):
            if reach > 3:
                last_pass(
                    s, [(3 - reach, reach - 3, g_low), (slab, reach - 3, g_high)], False
                )

        at_step(t, last_sides)

    def tick(i, _):
        late = i - count

        @pl.when(late >= 0)
        def _():
            second_half(late // count, late % count)

        @pl.when(i < units)
        def _():
            first_half(i // count, i % count)

        scan = i - 2

        @pl.when(scan == 0)
        def _():
            passages_here()

        @pl.when(jnp.logical_and(scan >= 0, scan < units))
        def _():
            own_scan(scan // count, scan % count)

        return 0

    lax.fori_loop(0, units + count, tick, 0)

    for direction in range(2):
        @pl.when(has[direction])
        def _():
            side_copy(direction).wait_send()
            for s in range(count):
                halo_copy(s, direction).wait_send()
    for i, target in enumerate(owners):
        @pl.when(me != target)
        def _():
            pass_copy(i).wait_send()
    for t in range(STEPS):
        for chain in range(chains):
            @pl.when(me != owner(chain))
            def _():
                emit_copy(t, chain).wait_send()

            @pl.when(me == owner(chain))
            def _():
                def left(i, _):
                    scan_copy(t, chain // 2, chain % 2, lax.rem(me + i, n)).wait_send()
                    return 0

                lax.fori_loop(1, n, left, 0)


def local(n, sources, plan, absorb, labels, kk, damp, guess):
    count, slab, height, breadth = guess.shape[1:]
    chains = 2 * count
    slots = 1 if n >= chains else chains
    tile = (height, breadth)
    planes = slab + 2 * HALO
    f32 = jnp.float32
    dma = pltpu.SemaphoreType.DMA
    hbm = pl.BlockSpec(memory_space=pltpu.HBM)
    owners = len({(c * n) // chains for c in range(chains)})
    scratch = [
        pltpu.VMEM((count, 2, planes) + tile, f32),
        pltpu.VMEM((count, 2, planes) + tile, f32),
        pltpu.VMEM((2, planes) + tile, f32),
        pltpu.VMEM((2, slab + 1) + tile, f32),
        pltpu.VMEM((2, 2, HALO - 1) + tile, f32),
        pltpu.VMEM((2, 2, HALO - 1) + tile, f32),
        pltpu.VMEM((2,) + tile, f32),
        pltpu.VMEM((2, 2) + tile, f32),
        pltpu.VMEM((STEPS, chains, 2) + tile, f32),
        pltpu.VMEM((STEPS, slots, n, 2) + tile, f32),
        pltpu.VMEM((STEPS, slots, n + 1, 2) + tile, f32),
        pltpu.VMEM((STEPS, count, 2, 2, 2) + tile, f32),
        pltpu.VMEM((n, 2) + tile, f32),
        pltpu.VMEM(sources.shape, f32),
        pltpu.SMEM(plan.shape, jnp.int32),
        pltpu.VMEM(absorb.shape, f32),
        pltpu.VMEM(labels.shape, jnp.int32),
        pltpu.SMEM(kk.shape, f32),
        pltpu.SMEM(damp.shape, jnp.int32),
        dma((6,)),
        dma((count,)),
        dma((count, 2)),
        dma((count, 2)),
        dma((2,)),
        dma((2,)),
        dma((owners,)),
        dma,
        dma((STEPS, chains)),
        dma((STEPS, slots)),
        dma((STEPS, slots, n)),
        dma((STEPS, count, 2)),
    ]
    return pl.pallas_call(
        functools.partial(kernel, n, slots),
        out_shape=jax.ShapeDtypeStruct(guess.shape, f32),
        in_specs=[hbm] * 7,
        out_specs=pl.BlockSpec(memory_space=pltpu.VMEM),
        scratch_shapes=scratch,
        compiler_params=pltpu.CompilerParams(
            collective_id=0, has_side_effects=True, vmem_limit_bytes=60 * 2**20
        ),
        cost_estimate=pl.CostEstimate(
            flops=300 * guess.size, bytes_accessed=8 * guess.size, transcendentals=0
        ),
    )(sources, plan, absorb, labels, kk, damp, guess)


def solution(mesh):
    return jax.shard_map(
        functools.partial(local, mesh.shape["depth"]),
        mesh=mesh,
        in_specs=(
            P(None, "groups", None, None),
            P("groups"),
            P("depth", "groups", None),
            P("depth", "groups", None),
            P(),
            P("groups"),
            P(None, "groups", "depth", None, None),
        ),
        out_specs=P(None, "groups", "depth", None, None),
        check_vma=False,
    )
```

```python
import functools

import jax
import jax.numpy as jnp
from jax import lax
from jax.experimental import pallas as pl
from jax.experimental.pallas import tpu as pltpu
from jax.sharding import PartitionSpec as P

STEPS = 2
HALO = 3 * STEPS
CHUNK = 16

relax_weight = 0.8
shift_ratio = 0.5
damping = 3.0
coupling = 0.25


def cmul(a, b):
    return (a[0] * b[0] - a[1] * b[1], a[0] * b[1] + a[1] * b[0])


def cadd(a, b):
    return (a[0] + b[0], a[1] + b[1])


def kernel(
    n, chains_of, sources_in, plan_in, absorb_in, labels_in, kk_in, damp_in, guess, out,
    field, work, inner, power, side_next, side_prev, own, side, emits, gathered, scanned,
    incoming, passages, pairing, sources, plan, absorb, labels, kk, damp, arg_sem, local_sem, halo_send, halo_recv, side_send, side_recv, pass_send,
    pass_recv, emit_send, emit_recv, scan_send, scan_recv,
):
    me = lax.axis_index("depth")
    count = guess.shape[1]
    slab = guess.shape[2]
    height, breadth = guess.shape[3:]
    wing = HALO - 1
    chains = 2 * count

    def owner(chain):
        return (chain * n) // chains

    def slot(chain):
        return 0 if chains_of == 1 else chain

    owners = sorted({(c * n) // chains for c in range(chains)})

    barrier = pltpu.get_barrier_semaphore()

    def greet(i, _):
        pl.semaphore_signal(
            barrier, inc=1, device_id={"depth": lax.rem(me + i, n)},
            device_id_type=pl.DeviceIdType.MESH,
        )
        return 0

    lax.fori_loop(1, n, greet, 0)

    def load(s):
        return pltpu.make_async_copy(
            guess.at[:, s], field.at[s, :, pl.ds(HALO, slab)], local_sem.at[s]
        )

    fetches = [
        pltpu.make_async_copy(there, here, arg_sem.at[i])
        for i, (there, here) in enumerate(
            (
                (labels_in, labels), (kk_in, kk), (damp_in, damp), (absorb_in, absorb),
                (plan_in, plan), (sources_in, sources),
            )
        )
    ]
    for fetch in fetches:
        fetch.start()
    for s in range(count):
        load(s).start()
    for fetch in fetches:
        fetch.wait()

    label = labels[0]
    squared = jnp.zeros((height, breadth), jnp.float32)
    for r in range(kk.shape[0]):
        squared = squared + jnp.where(label == r, kk[r], 0.0)
    rows = lax.broadcasted_iota(jnp.int32, (height, breadth), 0)
    lanes = lax.broadcasted_iota(jnp.int32, (height, breadth), 1)
    number = rows * breadth + lanes

    def mark(i, layer):
        return jnp.where(number == damp[i], 1.0, layer)

    layer = lax.fori_loop(
        0, damp.shape[0], mark, jnp.zeros((height, breadth), jnp.float32), unroll=8
    )
    own[0] = squared
    own[1] = absorb[0]

    pl.semaphore_wait(barrier, n - 1)

    def remote(src, dst, send, recv, target):
        return pltpu.make_async_remote_copy(
            src_ref=src, dst_ref=dst, send_sem=send, recv_sem=recv,
            device_id={"depth": target}, device_id_type=pl.DeviceIdType.MESH,
        )

    def side_copy(direction):
        return remote(
            own, side.at[1 - direction], side_send.at[direction], side_recv.at[1 - direction],
            me + (2 * direction - 1),
        )

    def halo_copy(s, direction):
        first = slab - HALO if direction else 0
        landing = 0 if direction else slab + HALO
        return remote(
            guess.at[:, s, pl.ds(first, HALO)], field.at[s, :, pl.ds(landing, HALO)],
            halo_send.at[s, direction], halo_recv.at[s, 1 - direction],
            me + (2 * direction - 1),
        )

    has = (me > 0, me < n - 1)
    for direction in range(2):
        @pl.when(has[direction])
        def _():
            side_copy(direction).start()
            for s in range(count):
                halo_copy(s, direction).start()

        @pl.when(jnp.logical_not(has[direction]))
        def _():
            side[direction] = jnp.zeros_like(side[direction])
            landing = slab + HALO if direction else 0
            for s in range(count):
                field[s, :, pl.ds(landing, HALO)] = jnp.zeros(
                    (2, HALO, height, breadth), jnp.float32
                )

    def wave(sq, ab):
        magnitude = jnp.exp(-ab / slab)
        phase = jnp.sqrt(sq)
        return (magnitude * jnp.cos(phase), magnitude * jnp.sin(phase))

    def relaxer(sq):
        real = 6.0 - sq
        imag = shift_ratio * sq + damping * layer
        size = real * real + imag * imag
        return (relax_weight * (real / size), relax_weight * (-imag / size))

    a_own = wave(squared, absorb[0])
    table = {0: (jnp.ones_like(squared), jnp.zeros_like(squared)), 1: a_own}
    power[0, 0], power[1, 0] = table[0]
    power[0, 1], power[1, 1] = a_own
    top = 1
    while top < slab:
        more = min(top, slab - top)
        head = (power[0, top], power[1, top])
        for j in range(1, more + 1):
            power[0, top + j], power[1, top + j] = cmul(head, (power[0, j], power[1, j]))
        top += more
    passage = (power[0, slab], power[1, slab])

    def pass_copy(i):
        return remote(
            power.at[:, slab], passages.at[me], pass_send.at[i], pass_recv, owners[i]
        )

    for i, target in enumerate(owners):
        @pl.when(me != target)
        def _():
            pass_copy(i).start()

        @pl.when(me == target)
        def _():
            passages[me, 0], passages[me, 1] = passage

    for direction in range(2):
        @pl.when(has[direction])
        def _():
            side_copy(1 - direction).wait_recv()

    damped = damping * layer
    real_own = 6.0 - squared
    g_own = relaxer(squared)
    media = []
    for direction in range(2):
        sq = side[direction, 0]
        inside = jnp.where(has[direction], 1.0, 0.0)
        g = relaxer(sq)
        a = wave(sq, side[direction, 1])

        def raised(k, a=a):
            total = None
            base = a
            while k:
                if k & 1:
                    total = base if total is None else cmul(total, base)
                k >>= 1
                if k:
                    base = cmul(base, base)
            return total

        low = a
        high = raised(slab - wing + 1)
        for i in range(wing):
            if direction == 0:
                side_next[0, 0, i], side_next[0, 1, i] = high
                side_prev[0, 0, wing - 1 - i], side_prev[0, 1, wing - 1 - i] = low
            else:
                side_next[1, 0, i], side_next[1, 1, i] = low
                side_prev[1, 0, wing - 1 - i], side_prev[1, 1, wing - 1 - i] = high
            low = cmul(low, a)
            high = cmul(high, a)
        media.append((6.0 - sq, (inside * g[0], inside * g[1])))

    keep_up, keep_down = rows > 0, rows < height - 1
    keep_left, keep_right = lanes > 0, lanes < breadth - 1

    def lateral(x):
        up = jnp.where(keep_up, pltpu.roll(x, 1, 0), 0.0)
        down = jnp.where(keep_down, pltpu.roll(x, height - 1, 0), 0.0)
        left = jnp.where(keep_left, pltpu.roll(x, 1, 1), 0.0)
        right = jnp.where(keep_right, pltpu.roll(x, breadth - 1, 1), 0.0)
        return (up + down) + (left + right)

    def vertical(x):
        up = jnp.where(keep_up, pltpu.roll(x, 1, 0), 0.0)
        down = jnp.where(keep_down, pltpu.roll(x, height - 1, 0), 0.0)
        return up + down

    gap = lax.broadcasted_iota(jnp.int32, (breadth, breadth), 0) - lax.broadcasted_iota(
        jnp.int32, (breadth, breadth), 1
    )
    pairing[...] = jnp.where(jnp.logical_or(gap == 1, gap == -1), 1.0, 0.0).astype(
        jnp.bfloat16
    )

    def window(ref, lead, first, planes):
        tiles = [
            [ref[lead + (c, first - 1 + j)] for j in range(planes + 2)] for c in range(2)
        ]
        if planes < CHUNK:
            return [(tiles[c], None) for c in range(2)]
        both = []
        for c in range(2):
            flat = ref[lead + (c, pl.ds(first, planes))].reshape(planes * height, breadth)
            coarse = flat.astype(jnp.bfloat16)
            fine = (flat - coarse.astype(jnp.float32)).astype(jnp.bfloat16)
            total = jnp.dot(coarse, pairing[...], preferred_element_type=jnp.float32)
            total += jnp.dot(fine, pairing[...], preferred_element_type=jnp.float32)
            both.append(
                (tiles[c], [total[j * height : (j + 1) * height] for j in range(planes)])
            )
        return both

    def beside(win, j):
        return tuple(
            w[j] + w[j + 2]
            + (lateral(w[j + 1]) if pairs is None else vertical(w[j + 1]) + pairs[j])
            for w, pairs in win
        )

    def residual_pass(s, parts, tally):
        wins = [window(field, (s,), part[0] + HALO, part[1]) for part in parts]
        source = (sources[0, s], sources[1, s])
        spot = plan[s] - me * slab
        results = []
        for (first, planes, real), win in zip(parts, wins):
            for j in range(planes):
                value = (win[0][0][j + 1], win[1][0][j + 1])
                near = beside(win, j)
                hit = jnp.where(spot == first + j, 1.0, 0.0)
                res = (
                    hit * source[0] + (near[0] - real * value[0] + damped * value[1]),
                    hit * source[1] + (near[1] - real * value[1] - damped * value[0]),
                )
                results.append((first + HALO + j, res))
                if tally is not None:
                    k = first + j
                    ahead = (power[0, slab - 1 - k], power[1, slab - 1 - k])
                    behind = (power[0, k], power[1, k])
                    tally = (
                        cadd(tally[0], cmul(ahead, res)), cadd(tally[1], cmul(behind, res))
                    )
        for at, res in results:
            work[s, 0, at], work[s, 1, at] = res
        return tally

    def start_pass(s, parts):
        results = []
        for first, planes, g, toward, from_low, from_high in parts:
            for j in range(planes):
                at = first + HALO + j
                up, down = toward(first + j)
                c = cadd(
                    (work[s, 0, at], work[s, 1, at]),
                    cadd(cmul(up, from_low), cmul(down, from_high)),
                )
                results.append((at, cmul(g, c)))
        for at, value in results:
            work[s, 0, at], work[s, 1, at] = value

    def middle_pass(s, parts):
        wins = [window(work, (s,), part[0] + HALO, part[1]) for part in parts]
        results = []
        for (first, planes, g), win in zip(parts, wins):
            for j in range(planes):
                moved = cmul(g, beside(win, j))
                results.append(
                    (
                        first + HALO + j,
                        [(2.0 - relax_weight) * win[c][0][j + 1] + moved[c] for c in range(2)],
                    )
                )
        for at, value in results:
            inner[0, at], inner[1, at] = value

    def last_pass(s, parts, final):
        wins = [window(inner, (), part[0] + HALO, part[1]) for part in parts]
        results = []
        for (first, planes, g), win in zip(parts, wins):
            for j in range(planes):
                at = first + HALO + j
                moved = cmul(g, beside(win, j))
                results.append(
                    (
                        first + j,
                        [
                            (field[s, c, at] + work[s, c, at])
                            + ((1.0 - relax_weight) * win[c][0][j + 1] + moved[c])
                            for c in range(2)
                        ],
                    )
                )
        for at, value in results:
            field[s, 0, at + HALO], field[s, 1, at + HALO] = value
            if final:
                out[0, s, at], out[1, s, at] = value

    def emit_copy(t, chain):
        return remote(
            emits.at[t, chain], gathered.at[t, slot(chain), me], emit_send.at[t, chain],
            emit_recv.at[t, slot(chain)], owner(chain),
        )

    def scan_copy(t, s, direction, target):
        here = slot(2 * s + direction)
        return remote(
            scanned.at[t, here, pl.ds(target, 2)], incoming.at[t, s, direction],
            scan_send.at[t, here, target], scan_recv.at[t, s, direction], target,
        )

    def own_scan(t, s):
        for direction in range(2):
            chain = 2 * s + direction
            here = slot(chain)

            @pl.when(me == owner(chain))
            def _():
                if n > 1:
                    every = gathered.at[t, here, pl.ds(0, n - 1)]
                    pltpu.make_async_copy(every, every, emit_recv.at[t, here]).wait()
                zero = jnp.zeros((height, breadth), jnp.float32)
                edge = direction * n
                scanned[t, here, edge, 0] = zero
                scanned[t, here, edge, 1] = zero

                def one(i, state):
                    at = n - 1 - i if direction else i
                    to = at + 1 - direction
                    scanned[t, here, to, 0] = state[0]
                    scanned[t, here, to, 1] = state[1]
                    return cadd(
                        cmul((passages[at, 0], passages[at, 1]), state),
                        (gathered[t, here, at, 0], gathered[t, here, at, 1]),
                    )

                lax.fori_loop(0, n, one, (zero, zero), unroll=4)

                def give(i, _):
                    scan_copy(t, s, direction, lax.rem(me + i, n)).start()
                    return 0

                lax.fori_loop(1, n, give, 0)
                incoming[t, s, direction] = scanned[t, here, pl.ds(me, 2)]

    pieces = slab // CHUNK
    units = STEPS * count

    def at_step(t, body):
        for step in range(STEPS):
            @pl.when(t == step)
            def _():
                body(3 * (STEPS - step))

    def first_half(t, s):
        @pl.when(t == 0)
        def _():
            load(s).wait()
            for direction in range(2):
                @pl.when(has[direction])
                def _():
                    halo_copy(s, 1 - direction).wait_recv()

        zero = jnp.zeros((height, breadth), jnp.float32)
        tally = lax.fori_loop(
            0, pieces,
            lambda i, tally: residual_pass(s, [(i * CHUNK, CHUNK, real_own)], tally),
            ((zero, zero), (zero, zero)),
        )
        for direction in range(2):
            chain = 2 * s + direction
            emits[t, chain, 0], emits[t, chain, 1] = tally[direction]

            @pl.when(me != owner(chain))
            def _():
                emit_copy(t, chain).start()

            @pl.when(me == owner(chain))
            def _():
                gathered[t, slot(chain), me, 0] = tally[direction][0]
                gathered[t, slot(chain), me, 1] = tally[direction][1]

        def sides(reach):
            residual_pass(
                s, [(1 - reach, reach - 1, media[0][0]), (slab, reach - 1, media[1][0])], None
            )

        at_step(t, sides)

    def passages_here():
        for target in owners:
            @pl.when(me == target)
            def _():
                if n > 1:
                    every = passages.at[pl.ds(0, n - 1)]
                    pltpu.make_async_copy(every, every, pass_recv).wait()

    def second_half(t, s):
        for direction in range(2):
            @pl.when(me != owner(2 * s + direction))
            def _():
                scan_copy(t, s, direction, me).wait_recv()

        def arrived(direction, i):
            return (incoming[t, s, direction, i, 0], incoming[t, s, direction, i, 1])

        def emitted(direction):
            return (emits[t, 2 * s + direction, 0], emits[t, 2 * s + direction, 1])

        def scaled(z):
            return (coupling * z[0], coupling * z[1])

        through = (power[0, slab], power[1, slab])
        next_low, next_own = arrived(0, 0), arrived(0, 1)
        prev_own, prev_high = arrived(1, 0), arrived(1, 1)
        next_high = scaled(cadd(cmul(through, next_own), emitted(0)))
        prev_low = scaled(cadd(cmul(through, prev_own), emitted(1)))
        next_low, next_own = scaled(next_low), scaled(next_own)
        prev_own, prev_high = scaled(prev_own), scaled(prev_high)

        def toward_own(k):
            return (
                (power[0, k + 1], power[1, k + 1]),
                (power[0, slab - k], power[1, slab - k]),
            )

        def toward_side(direction):
            def get(k):
                i = k - slab if direction else k + wing
                return (
                    (side_next[direction, 0, i], side_next[direction, 1, i]),
                    (side_prev[direction, 0, i], side_prev[direction, 1, i]),
                )
            return get

        g_low, g_high = media[0][1], media[1][1]

        def walk(body):
            lax.fori_loop(0, pieces, lambda i, _: (body(i * CHUNK), 0)[1], 0)

        walk(
            lambda k: start_pass(s, [(k, CHUNK, g_own, toward_own, next_own, prev_own)])
        )

        def start_sides(reach):
            start_pass(
                s,
                [
                    (1 - reach, reach - 1, g_low, toward_side(0), next_low, prev_low),
                    (slab, reach - 1, g_high, toward_side(1), next_high, prev_high),
                ],
            )
            middle_pass(s, [(2 - reach, reach - 2, g_low), (slab, reach - 2, g_high)])

        at_step(t, start_sides)
        walk(lambda k: middle_pass(s, [(k, CHUNK, g_own)]))
        walk(lambda k: last_pass(s, [(k, CHUNK, g_own)], True))

        def last_sides(reach):
            if reach > 3:
                last_pass(
                    s, [(3 - reach, reach - 3, g_low), (slab, reach - 3, g_high)], False
                )

        at_step(t, last_sides)

    def tick(i, _):
        late = i - count

        @pl.when(late >= 0)
        def _():
            second_half(late // count, late % count)

        @pl.when(i < units)
        def _():
            first_half(i // count, i % count)

        scan = i - 2

        @pl.when(scan == 0)
        def _():
            passages_here()

        @pl.when(jnp.logical_and(scan >= 0, scan < units))
        def _():
            own_scan(scan // count, scan % count)

        return 0

    lax.fori_loop(0, units + count, tick, 0)

    for direction in range(2):
        @pl.when(has[direction])
        def _():
            side_copy(direction).wait_send()
            for s in range(count):
                halo_copy(s, direction).wait_send()
    for i, target in enumerate(owners):
        @pl.when(me != target)
        def _():
            pass_copy(i).wait_send()
    for t in range(STEPS):
        for chain in range(chains):
            @pl.when(me != owner(chain))
            def _():
                emit_copy(t, chain).wait_send()

            @pl.when(me == owner(chain))
            def _():
                def left(i, _):
                    scan_copy(t, chain // 2, chain % 2, lax.rem(me + i, n)).wait_send()
                    return 0

                lax.fori_loop(1, n, left, 0)


def local(n, sources, plan, absorb, labels, kk, damp, guess):
    count, slab, height, breadth = guess.shape[1:]
    chains = 2 * count
    slots = 1 if n >= chains else chains
    tile = (height, breadth)
    planes = slab + 2 * HALO
    f32 = jnp.float32
    dma = pltpu.SemaphoreType.DMA
    hbm = pl.BlockSpec(memory_space=pltpu.HBM)
    owners = len({(c * n) // chains for c in range(chains)})
    scratch = [
        pltpu.VMEM((count, 2, planes) + tile, f32),
        pltpu.VMEM((count, 2, planes) + tile, f32),
        pltpu.VMEM((2, planes) + tile, f32),
        pltpu.VMEM((2, slab + 1) + tile, f32),
        pltpu.VMEM((2, 2, HALO - 1) + tile, f32),
        pltpu.VMEM((2, 2, HALO - 1) + tile, f32),
        pltpu.VMEM((2,) + tile, f32),
        pltpu.VMEM((2, 2) + tile, f32),
        pltpu.VMEM((STEPS, chains, 2) + tile, f32),
        pltpu.VMEM((STEPS, slots, n, 2) + tile, f32),
        pltpu.VMEM((STEPS, slots, n + 1, 2) + tile, f32),
        pltpu.VMEM((STEPS, count, 2, 2, 2) + tile, f32),
        pltpu.VMEM((n, 2) + tile, f32),
        pltpu.VMEM((breadth, breadth), jnp.bfloat16),
        pltpu.VMEM(sources.shape, f32),
        pltpu.SMEM(plan.shape, jnp.int32),
        pltpu.VMEM(absorb.shape, f32),
        pltpu.VMEM(labels.shape, jnp.int32),
        pltpu.SMEM(kk.shape, f32),
        pltpu.SMEM(damp.shape, jnp.int32),
        dma((6,)),
        dma((count,)),
        dma((count, 2)),
        dma((count, 2)),
        dma((2,)),
        dma((2,)),
        dma((owners,)),
        dma,
        dma((STEPS, chains)),
        dma((STEPS, slots)),
        dma((STEPS, slots, n)),
        dma((STEPS, count, 2)),
    ]
    return pl.pallas_call(
        functools.partial(kernel, n, slots),
        out_shape=jax.ShapeDtypeStruct(guess.shape, f32),
        in_specs=[hbm] * 7,
        out_specs=pl.BlockSpec(memory_space=pltpu.VMEM),
        scratch_shapes=scratch,
        compiler_params=pltpu.CompilerParams(
            collective_id=0, has_side_effects=True, vmem_limit_bytes=60 * 2**20
        ),
        cost_estimate=pl.CostEstimate(
            flops=300 * guess.size, bytes_accessed=8 * guess.size, transcendentals=0
        ),
    )(sources, plan, absorb, labels, kk, damp, guess)


def solution(mesh):
    return jax.shard_map(
        functools.partial(local, mesh.shape["depth"]),
        mesh=mesh,
        in_specs=(
            P(None, "groups", None, None),
            P("groups"),
            P("depth", "groups", None),
            P("depth", "groups", None),
            P(),
            P("groups"),
            P(None, "groups", "depth", None, None),
        ),
        out_specs=P(None, "groups", "depth", None, None),
        check_vma=False,
    )
```

```python
import functools

import jax
import jax.numpy as jnp
from jax import lax
from jax.experimental import pallas as pl
from jax.experimental.pallas import tpu as pltpu
from jax.sharding import PartitionSpec as P

STEPS = 2
HALO = 3 * STEPS
CHUNK = 16

relax_weight = 0.8
shift_ratio = 0.5
damping = 3.0
coupling = 0.25


def cmul(a, b):
    return (a[0] * b[0] - a[1] * b[1], a[0] * b[1] + a[1] * b[0])


def cadd(a, b):
    return (a[0] + b[0], a[1] + b[1])


def kernel(
    n, chains_of, sources_in, plan_in, absorb_in, labels_in, kk_in, damp_in, guess, out,
    field, work, inner, power, side_next, side_prev, own, side, emits, gathered, scanned,
    incoming, passages, sources, plan, absorb, labels, kk, damp, arg_sem, local_sem, halo_send, halo_recv, side_send, side_recv, pass_send,
    pass_recv, emit_send, emit_recv, scan_send, scan_recv,
):
    me = lax.axis_index("depth")
    count = guess.shape[1]
    slab = guess.shape[2]
    height, breadth = guess.shape[3:]
    wing = HALO - 1
    chains = 2 * count

    def owner(chain):
        return (chain * n) // chains

    def slot(chain):
        return 0 if chains_of == 1 else chain

    owners = sorted({(c * n) // chains for c in range(chains)})

    barrier = pltpu.get_barrier_semaphore()

    def greet(i, _):
        pl.semaphore_signal(
            barrier, inc=1, device_id={"depth": lax.rem(me + i, n)},
            device_id_type=pl.DeviceIdType.MESH,
        )
        return 0

    lax.fori_loop(1, n, greet, 0)

    def load(s):
        return pltpu.make_async_copy(
            guess.at[:, s], field.at[s, :, pl.ds(HALO, slab)], local_sem.at[s]
        )

    fetches = [
        pltpu.make_async_copy(there, here, arg_sem.at[i])
        for i, (there, here) in enumerate(
            (
                (labels_in, labels), (kk_in, kk), (damp_in, damp), (absorb_in, absorb),
                (plan_in, plan), (sources_in, sources),
            )
        )
    ]
    for fetch in fetches:
        fetch.start()
    for s in range(count):
        load(s).start()
    for fetch in fetches:
        fetch.wait()

    label = labels[0]
    squared = jnp.zeros((height, breadth), jnp.float32)
    for r in range(kk.shape[0]):
        squared = squared + jnp.where(label == r, kk[r], 0.0)
    rows = lax.broadcasted_iota(jnp.int32, (height, breadth), 0)
    lanes = lax.broadcasted_iota(jnp.int32, (height, breadth), 1)
    number = rows * breadth + lanes

    def mark(i, layer):
        return jnp.where(number == damp[i], 1.0, layer)

    layer = lax.fori_loop(
        0, damp.shape[0], mark, jnp.zeros((height, breadth), jnp.float32), unroll=8
    )
    own[0] = squared
    own[1] = absorb[0]

    pl.semaphore_wait(barrier, n - 1)

    def remote(src, dst, send, recv, target):
        return pltpu.make_async_remote_copy(
            src_ref=src, dst_ref=dst, send_sem=send, recv_sem=recv,
            device_id={"depth": target}, device_id_type=pl.DeviceIdType.MESH,
        )

    def side_copy(direction):
        return remote(
            own, side.at[1 - direction], side_send.at[direction], side_recv.at[1 - direction],
            me + (2 * direction - 1),
        )

    def halo_copy(s, direction):
        first = slab - HALO if direction else 0
        landing = 0 if direction else slab + HALO
        return remote(
            guess.at[:, s, pl.ds(first, HALO)], field.at[s, :, pl.ds(landing, HALO)],
            halo_send.at[s, direction], halo_recv.at[s, 1 - direction],
            me + (2 * direction - 1),
        )

    has = (me > 0, me < n - 1)
    for direction in range(2):
        @pl.when(has[direction])
        def _():
            side_copy(direction).start()
            for s in range(count):
                halo_copy(s, direction).start()

        @pl.when(jnp.logical_not(has[direction]))
        def _():
            side[direction] = jnp.zeros_like(side[direction])
            landing = slab + HALO if direction else 0
            for s in range(count):
                field[s, :, pl.ds(landing, HALO)] = jnp.zeros(
                    (2, HALO, height, breadth), jnp.float32
                )

    def wave(sq, ab):
        magnitude = jnp.exp(-ab / slab)
        phase = jnp.sqrt(sq)
        return (magnitude * jnp.cos(phase), magnitude * jnp.sin(phase))

    def relaxer(sq):
        real = 6.0 - sq
        imag = shift_ratio * sq + damping * layer
        size = real * real + imag * imag
        return (relax_weight * (real / size), relax_weight * (-imag / size))

    a_own = wave(squared, absorb[0])
    table = {0: (jnp.ones_like(squared), jnp.zeros_like(squared)), 1: a_own}
    power[0, 0], power[1, 0] = table[0]
    power[0, 1], power[1, 1] = a_own
    top = 1
    while top < slab:
        more = min(top, slab - top)
        head = (power[0, top], power[1, top])
        for j in range(1, more + 1):
            power[0, top + j], power[1, top + j] = cmul(head, (power[0, j], power[1, j]))
        top += more
    passage = (power[0, slab], power[1, slab])

    def pass_copy(i):
        return remote(
            power.at[:, slab], passages.at[me], pass_send.at[i], pass_recv, owners[i]
        )

    for i, target in enumerate(owners):
        @pl.when(me != target)
        def _():
            pass_copy(i).start()

        @pl.when(me == target)
        def _():
            passages[me, 0], passages[me, 1] = passage

    for direction in range(2):
        @pl.when(has[direction])
        def _():
            side_copy(1 - direction).wait_recv()

    damped = damping * layer
    real_own = 6.0 - squared
    g_own = relaxer(squared)
    media = []
    for direction in range(2):
        sq = side[direction, 0]
        inside = jnp.where(has[direction], 1.0, 0.0)
        g = relaxer(sq)
        a = wave(sq, side[direction, 1])

        def raised(k, a=a):
            total = None
            base = a
            while k:
                if k & 1:
                    total = base if total is None else cmul(total, base)
                k >>= 1
                if k:
                    base = cmul(base, base)
            return total

        low = a
        high = raised(slab - wing + 1)
        for i in range(wing):
            if direction == 0:
                side_next[0, 0, i], side_next[0, 1, i] = high
                side_prev[0, 0, wing - 1 - i], side_prev[0, 1, wing - 1 - i] = low
            else:
                side_next[1, 0, i], side_next[1, 1, i] = low
                side_prev[1, 0, wing - 1 - i], side_prev[1, 1, wing - 1 - i] = high
            low = cmul(low, a)
            high = cmul(high, a)
        media.append((6.0 - sq, (inside * g[0], inside * g[1])))

    keep_up, keep_down = rows > 0, rows < height - 1
    keep_left, keep_right = lanes > 0, lanes < breadth - 1

    def lateral(x):
        up = jnp.where(keep_up, pltpu.roll(x, 1, 0), 0.0)
        down = jnp.where(keep_down, pltpu.roll(x, height - 1, 0), 0.0)
        left = jnp.where(keep_left, pltpu.roll(x, 1, 1), 0.0)
        right = jnp.where(keep_right, pltpu.roll(x, breadth - 1, 1), 0.0)
        return (up + down) + (left + right)

    def window(ref, lead, first, planes):
        view = ref.at[lead + (slice(None), pl.ds(first - 1, planes + 2))]
        return [[view[c, j] for j in range(planes + 2)] for c in range(2)]

    def beside(win, j):
        return tuple(w[j] + w[j + 2] + lateral(w[j + 1]) for w in win)

    def residual_pass(s, parts, tally):
        wins = [window(field, (s,), part[0] + HALO, part[1]) for part in parts]
        source = (sources[0, s], sources[1, s])
        spot = plan[s] - me * slab
        results = []
        for (first, planes, real), win in zip(parts, wins):
            view = work.at[s, :, pl.ds(first + HALO, planes)]
            if tally is not None:
                far = power.at[:, pl.ds(slab - first - planes, planes)]
                near_by = power.at[:, pl.ds(first, planes)]
            for j in range(planes):
                value = (win[0][j + 1], win[1][j + 1])
                near = beside(win, j)
                hit = jnp.where(spot == first + j, 1.0, 0.0)
                res = (
                    hit * source[0] + (near[0] - real * value[0] + damped * value[1]),
                    hit * source[1] + (near[1] - real * value[1] - damped * value[0]),
                )
                results.append((view, j, res))
                if tally is not None:
                    ahead = (far[0, planes - 1 - j], far[1, planes - 1 - j])
                    behind = (near_by[0, j], near_by[1, j])
                    tally = (
                        cadd(tally[0], cmul(ahead, res)), cadd(tally[1], cmul(behind, res))
                    )
        for view, j, res in results:
            view[0, j], view[1, j] = res
        return tally

    def start_pass(s, parts):
        results = []
        for first, planes, g, toward, from_low, from_high in parts:
            view = work.at[s, :, pl.ds(first + HALO, planes)]
            coefficient = toward(first, planes)
            for j in range(planes):
                up, down = coefficient(j)
                c = cadd(
                    (view[0, j], view[1, j]),
                    cadd(cmul(up, from_low), cmul(down, from_high)),
                )
                results.append((view, j, cmul(g, c)))
        for view, j, value in results:
            view[0, j], view[1, j] = value

    def middle_pass(s, parts):
        wins = [window(work, (s,), part[0] + HALO, part[1]) for part in parts]
        results = []
        for (first, planes, g), win in zip(parts, wins):
            view = inner.at[:, pl.ds(first + HALO, planes)]
            for j in range(planes):
                moved = cmul(g, beside(win, j))
                results.append(
                    (
                        view,
                        j,
                        [(2.0 - relax_weight) * win[c][j + 1] + moved[c] for c in range(2)],
                    )
                )
        for view, j, value in results:
            view[0, j], view[1, j] = value

    def last_pass(s, parts, final):
        wins = [window(inner, (), part[0] + HALO, part[1]) for part in parts]
        results = []
        for (first, planes, g), win in zip(parts, wins):
            view = field.at[s, :, pl.ds(first + HALO, planes)]
            begun = work.at[s, :, pl.ds(first + HALO, planes)]
            target = out.at[:, s, pl.ds(first, planes)] if final else None
            for j in range(planes):
                moved = cmul(g, beside(win, j))
                results.append(
                    (
                        view,
                        target,
                        j,
                        [
                            (view[c, j] + begun[c, j])
                            + ((1.0 - relax_weight) * win[c][j + 1] + moved[c])
                            for c in range(2)
                        ],
                    )
                )
        for view, target, j, value in results:
            view[0, j], view[1, j] = value
            if final:
                target[0, j], target[1, j] = value

    def emit_copy(t, chain):
        return remote(
            emits.at[t, chain], gathered.at[t, slot(chain), me], emit_send.at[t, chain],
            emit_recv.at[t, slot(chain)], owner(chain),
        )

    def scan_copy(t, s, direction, target):
        here = slot(2 * s + direction)
        return remote(
            scanned.at[t, here, pl.ds(target, 2)], incoming.at[t, s, direction],
            scan_send.at[t, here, target], scan_recv.at[t, s, direction], target,
        )

    def own_scan(t, s):
        for direction in range(2):
            chain = 2 * s + direction
            here = slot(chain)

            @pl.when(me == owner(chain))
            def _():
                if n > 1:
                    every = gathered.at[t, here, pl.ds(0, n - 1)]
                    pltpu.make_async_copy(every, every, emit_recv.at[t, here]).wait()
                zero = jnp.zeros((height, breadth), jnp.float32)
                edge = direction * n
                scanned[t, here, edge, 0] = zero
                scanned[t, here, edge, 1] = zero

                def one(i, state):
                    at = n - 1 - i if direction else i
                    to = at + 1 - direction
                    scanned[t, here, to, 0] = state[0]
                    scanned[t, here, to, 1] = state[1]
                    return cadd(
                        cmul((passages[at, 0], passages[at, 1]), state),
                        (gathered[t, here, at, 0], gathered[t, here, at, 1]),
                    )

                lax.fori_loop(0, n, one, (zero, zero), unroll=4)

                def give(i, _):
                    scan_copy(t, s, direction, lax.rem(me + i, n)).start()
                    return 0

                lax.fori_loop(1, n, give, 0)
                incoming[t, s, direction] = scanned[t, here, pl.ds(me, 2)]

    pieces = slab // CHUNK
    units = STEPS * count

    def at_step(t, body):
        for step in range(STEPS):
            @pl.when(t == step)
            def _():
                body(3 * (STEPS - step))

    def first_half(t, s):
        @pl.when(t == 0)
        def _():
            load(s).wait()
            for direction in range(2):
                @pl.when(has[direction])
                def _():
                    halo_copy(s, 1 - direction).wait_recv()

        zero = jnp.zeros((height, breadth), jnp.float32)
        tally = lax.fori_loop(
            0, pieces,
            lambda i, tally: residual_pass(s, [(i * CHUNK, CHUNK, real_own)], tally),
            ((zero, zero), (zero, zero)),
        )
        for direction in range(2):
            chain = 2 * s + direction
            emits[t, chain, 0], emits[t, chain, 1] = tally[direction]

            @pl.when(me != owner(chain))
            def _():
                emit_copy(t, chain).start()

            @pl.when(me == owner(chain))
            def _():
                gathered[t, slot(chain), me, 0] = tally[direction][0]
                gathered[t, slot(chain), me, 1] = tally[direction][1]

        def sides(reach):
            residual_pass(
                s, [(1 - reach, reach - 1, media[0][0]), (slab, reach - 1, media[1][0])], None
            )

        at_step(t, sides)

    def passages_here():
        for target in owners:
            @pl.when(me == target)
            def _():
                if n > 1:
                    every = passages.at[pl.ds(0, n - 1)]
                    pltpu.make_async_copy(every, every, pass_recv).wait()

    def second_half(t, s):
        for direction in range(2):
            @pl.when(me != owner(2 * s + direction))
            def _():
                scan_copy(t, s, direction, me).wait_recv()

        def arrived(direction, i):
            return (incoming[t, s, direction, i, 0], incoming[t, s, direction, i, 1])

        def emitted(direction):
            return (emits[t, 2 * s + direction, 0], emits[t, 2 * s + direction, 1])

        def scaled(z):
            return (coupling * z[0], coupling * z[1])

        through = (power[0, slab], power[1, slab])
        next_low, next_own = arrived(0, 0), arrived(0, 1)
        prev_own, prev_high = arrived(1, 0), arrived(1, 1)
        next_high = scaled(cadd(cmul(through, next_own), emitted(0)))
        prev_low = scaled(cadd(cmul(through, prev_own), emitted(1)))
        next_low, next_own = scaled(next_low), scaled(next_own)
        prev_own, prev_high = scaled(prev_own), scaled(prev_high)

        def toward_own(first, planes):
            up = power.at[:, pl.ds(first + 1, planes)]
            down = power.at[:, pl.ds(slab - first - planes + 1, planes)]
            back = planes - 1
            return lambda j: ((up[0, j], up[1, j]), (down[0, back - j], down[1, back - j]))

        def toward_side(direction):
            def get(first, planes):
                i = first - slab if direction else first + wing
                return lambda j: (
                    (side_next[direction, 0, i + j], side_next[direction, 1, i + j]),
                    (side_prev[direction, 0, i + j], side_prev[direction, 1, i + j]),
                )
            return get

        g_low, g_high = media[0][1], media[1][1]

        def walk(body):
            lax.fori_loop(0, pieces, lambda i, _: (body(i * CHUNK), 0)[1], 0)

        walk(
            lambda k: start_pass(s, [(k, CHUNK, g_own, toward_own, next_own, prev_own)])
        )

        def start_sides(reach):
            start_pass(
                s,
                [
                    (1 - reach, reach - 1, g_low, toward_side(0), next_low, prev_low),
                    (slab, reach - 1, g_high, toward_side(1), next_high, prev_high),
                ],
            )
            middle_pass(s, [(2 - reach, reach - 2, g_low), (slab, reach - 2, g_high)])

        at_step(t, start_sides)
        walk(lambda k: middle_pass(s, [(k, CHUNK, g_own)]))
        walk(lambda k: last_pass(s, [(k, CHUNK, g_own)], True))

        def last_sides(reach):
            if reach > 3:
                last_pass(
                    s, [(3 - reach, reach - 3, g_low), (slab, reach - 3, g_high)], False
                )

        at_step(t, last_sides)

    def tick(i, _):
        late = i - count

        @pl.when(late >= 0)
        def _():
            second_half(late // count, late % count)

        @pl.when(i < units)
        def _():
            first_half(i // count, i % count)

        scan = i - 2

        @pl.when(scan == 0)
        def _():
            passages_here()

        @pl.when(jnp.logical_and(scan >= 0, scan < units))
        def _():
            own_scan(scan // count, scan % count)

        return 0

    lax.fori_loop(0, units + count, tick, 0)

    for direction in range(2):
        @pl.when(has[direction])
        def _():
            side_copy(direction).wait_send()
            for s in range(count):
                halo_copy(s, direction).wait_send()
    for i, target in enumerate(owners):
        @pl.when(me != target)
        def _():
            pass_copy(i).wait_send()
    for t in range(STEPS):
        for chain in range(chains):
            @pl.when(me != owner(chain))
            def _():
                emit_copy(t, chain).wait_send()

            @pl.when(me == owner(chain))
            def _():
                def left(i, _):
                    scan_copy(t, chain // 2, chain % 2, lax.rem(me + i, n)).wait_send()
                    return 0

                lax.fori_loop(1, n, left, 0)


def local(n, sources, plan, absorb, labels, kk, damp, guess):
    count, slab, height, breadth = guess.shape[1:]
    chains = 2 * count
    slots = 1 if n >= chains else chains
    tile = (height, breadth)
    planes = slab + 2 * HALO
    f32 = jnp.float32
    dma = pltpu.SemaphoreType.DMA
    hbm = pl.BlockSpec(memory_space=pltpu.HBM)
    owners = len({(c * n) // chains for c in range(chains)})
    scratch = [
        pltpu.VMEM((count, 2, planes) + tile, f32),
        pltpu.VMEM((count, 2, planes) + tile, f32),
        pltpu.VMEM((2, planes) + tile, f32),
        pltpu.VMEM((2, slab + 1) + tile, f32),
        pltpu.VMEM((2, 2, HALO - 1) + tile, f32),
        pltpu.VMEM((2, 2, HALO - 1) + tile, f32),
        pltpu.VMEM((2,) + tile, f32),
        pltpu.VMEM((2, 2) + tile, f32),
        pltpu.VMEM((STEPS, chains, 2) + tile, f32),
        pltpu.VMEM((STEPS, slots, n, 2) + tile, f32),
        pltpu.VMEM((STEPS, slots, n + 1, 2) + tile, f32),
        pltpu.VMEM((STEPS, count, 2, 2, 2) + tile, f32),
        pltpu.VMEM((n, 2) + tile, f32),
        pltpu.VMEM(sources.shape, f32),
        pltpu.SMEM(plan.shape, jnp.int32),
        pltpu.VMEM(absorb.shape, f32),
        pltpu.VMEM(labels.shape, jnp.int32),
        pltpu.SMEM(kk.shape, f32),
        pltpu.SMEM(damp.shape, jnp.int32),
        dma((6,)),
        dma((count,)),
        dma((count, 2)),
        dma((count, 2)),
        dma((2,)),
        dma((2,)),
        dma((owners,)),
        dma,
        dma((STEPS, chains)),
        dma((STEPS, slots)),
        dma((STEPS, slots, n)),
        dma((STEPS, count, 2)),
    ]
    return pl.pallas_call(
        functools.partial(kernel, n, slots),
        out_shape=jax.ShapeDtypeStruct(guess.shape, f32),
        in_specs=[hbm] * 7,
        out_specs=pl.BlockSpec(memory_space=pltpu.VMEM),
        scratch_shapes=scratch,
        compiler_params=pltpu.CompilerParams(
            collective_id=0, has_side_effects=True, vmem_limit_bytes=60 * 2**20
        ),
        cost_estimate=pl.CostEstimate(
            flops=300 * guess.size, bytes_accessed=8 * guess.size, transcendentals=0
        ),
    )(sources, plan, absorb, labels, kk, damp, guess)


def solution(mesh):
    return jax.shard_map(
        functools.partial(local, mesh.shape["depth"]),
        mesh=mesh,
        in_specs=(
            P(None, "groups", None, None),
            P("groups"),
            P("depth", "groups", None),
            P("depth", "groups", None),
            P(),
            P("groups"),
            P(None, "groups", "depth", None, None),
        ),
        out_specs=P(None, "groups", "depth", None, None),
        check_vma=False,
    )
```
